32 devices in a mesh: probe: 2 (over x), slab: 16 (over z, y, core).
Axes of the slice: x: 2, y: 2, z: 4, core: 2. Of those that a mesh axis runs over, the one named last changes fastest.
Arguments:
- probes: float32 [3, 512, 16384], P(None, 'probe', 'slab'), may hold values from -6 to 6
- viscosity: float32 [16384], P('slab'), may hold values from 0.8 to 1.25
- coupling: float32 [4, 3, 3, 16384], P(None, None, None, 'slab'), may hold values from -0.06 to 0.06
- misfit_weight: float32 [3, 16384], P(None, 'slab'), may hold values from 0.7 to 1.4
- band_offsets: int32 [4], replicated, may hold values from -4 to 4, as said below
Outputs:
- basis: float32 [3, 512, 16384], P(None, 'probe', 'slab')
- r_factor: float32 [512, 512], P('probe')
The draws below stay inside these ranges and needn't reach their ends.
Inputs may be any that keep to these rules, and one draw needn't show every extreme that they name: `band_offsets`: 4 distinct nonzero offsets; both -4 and 4 are among them.
All inputs are finite; a program needn't handle non-finite values.
Results may differ from the reference program's by a relative error of at most 0.0003.
Values sent between devices are 32-bit elements; how exact they have to be, the bound alone decides.
No kernel may reach another device: no remote copies, remote signals or barrier semaphores. Data moves between devices by JAX's collectives and lax.ppermute only.
A program may use at most 64 MiB of HBM per device.

```python
import math
import jax
import jax.numpy as jnp
from jax import lax

PROBES = 512
REACH = 4
BANDS = 4
CELLS = 16384
ROWS = 49152


def draw_band_offsets(key, part):
    first_key, second_key = jax.random.split(key)
    candidates = jnp.concatenate([jnp.arange(1 - REACH, 0), jnp.arange(1, REACH)]).astype(jnp.int32)
    picked = jax.random.permutation(first_key, candidates)[:2]
    ends = jnp.array([0 - REACH, REACH], dtype=jnp.int32)
    return jax.random.permutation(second_key, jnp.concatenate([ends, picked]))


def level_of(rng, extent, cuts, smallest, largest):
    def one(position, shards_of):
        draws = jax.random.uniform(jax.random.fold_in(jax.random.fold_in(rng, 6), position), (shards_of,), jnp.float32, smallest / len(cuts), largest / len(cuts))
        return jnp.repeat(jnp.exp(draws), extent[position] // shards_of).reshape((-1,) + (1,) * (len(extent) - position - 1))

    factor_of = one(*cuts[0])
    for cut in cuts[1:]:
        factor_of = factor_of * one(*cut)
    return factor_of


def normal_values(key, dims, deviation, reach, pieces=(), kind=jnp.bfloat16):
    gain = level_of(key, dims, pieces, -0.22, 0.18) if pieces else 1.0
    values = jax.random.normal(key, dims, jnp.float32) * deviation * gain
    return jnp.minimum(jnp.maximum(values, -reach), reach).astype(kind)


def setup_inputs(seed: int = 0) -> dict:
    arg_keys = jax.random.split(jax.random.key(seed), 6)
    probes = normal_values(arg_keys[0], (3, PROBES, CELLS), 1.0, 6.0, ((1, 2), (2, 16)), jnp.float32)
    viscosity = jnp.clip(jnp.exp(math.log(1.25) - 0.4462871 * jax.random.uniform(arg_keys[1], (CELLS,), jnp.float32) ** level_of(arg_keys[1], (CELLS,), ((0, 16),), -0.2, 0.2)), 0.8, 1.25)
    coupling = jnp.clip(jax.random.uniform(arg_keys[2], (BANDS, 3, 3, CELLS), jnp.float32, -0.06, 0.06) * level_of(arg_keys[2], (BANDS, 3, 3, CELLS), ((3, 16),), -0.4, 0.0), -0.06, 0.06)
    misfit_weight = jnp.clip(jnp.exp(math.log(1.4) - 0.6931472 * jax.random.uniform(arg_keys[3], (3, CELLS), jnp.float32) ** level_of(arg_keys[3], (3, CELLS), ((1, 16),), -0.2, 0.2)), 0.7, 1.4)
    band_offsets = draw_band_offsets(jax.random.fold_in(arg_keys[5], 71), 0)
    return dict(probes=probes, viscosity=viscosity, coupling=coupling, misfit_weight=misfit_weight, band_offsets=band_offsets)


def small_cholesky(matrix):
    size = matrix.shape[0]
    places = jnp.arange(size, dtype=jnp.int32)

    def column_step(index, lower):
        row_j = lax.dynamic_index_in_dim(lower, index, 0, keepdims=False)
        col_a = lax.dynamic_index_in_dim(matrix, index, 1, keepdims=False)
        column = col_a - jnp.dot(lower, row_j, precision=lax.Precision.HIGHEST)
        pivot = jnp.sqrt(jnp.sum(jnp.where(places == index, column, 0.0)))
        filled = jnp.where(places > index, column / pivot, jnp.where(places == index, pivot, 0.0))
        marker = (places == index).astype(matrix.dtype)
        return lower + filled[:, None] * marker[None, :]
    return lax.fori_loop(0, size, column_step, jnp.zeros_like(matrix))

def small_lower_inverse(lower):
    size = lower.shape[0]
    places = jnp.arange(size, dtype=jnp.int32)

    def row_step(index, inverse):
        row_l = lax.dynamic_index_in_dim(lower, index, 0, keepdims=False)
        diag_value = jnp.sum(jnp.where(places == index, row_l, 0.0))
        marker = (places == index).astype(lower.dtype)
        strict = jnp.where(places < index, row_l, 0.0)
        new_row = (marker - jnp.dot(strict, inverse, precision=lax.Precision.HIGHEST)) / diag_value
        return inverse + marker[:, None] * new_row[None, :]
    return lax.fori_loop(0, size, row_step, jnp.zeros_like(lower))

def factorize(gram):
    size = gram.shape[0]
    width = 64
    count = size // width
    work = gram
    lower_blocks = {}
    inverse_diag = []
    for outer in range(count):
        lo = outer * width
        diag_block = work[lo:lo + width, lo:lo + width]
        diag_lower = small_cholesky(diag_block)
        diag_inverse = small_lower_inverse(diag_lower)
        lower_blocks[outer, outer] = diag_lower
        inverse_diag.append(diag_inverse)
        if outer + 1 < count:
            below = jnp.dot(work[lo + width:, lo:lo + width], diag_inverse.T, precision=lax.Precision.HIGHEST)
            for inner in range(outer + 1, count):
                start = (inner - outer - 1) * width
                lower_blocks[inner, outer] = below[start:start + width]
            trailing = work[lo + width:, lo + width:] - jnp.dot(below, below.T, precision=lax.Precision.HIGHEST)
            work = work.at[lo + width:, lo + width:].set(trailing)
    zero_block = jnp.zeros((width, width), dtype=gram.dtype)
    lower_rows = []
    for inner in range(count):
        lower_rows.append(jnp.concatenate([lower_blocks.get((inner, outer), zero_block) for outer in range(count)], 1))
    lower = jnp.concatenate(lower_rows, 0)
    inverse_blocks = {}
    for outer in range(count):
        inverse_blocks[outer, outer] = inverse_diag[outer]
        for inner in range(outer + 1, count):
            total = jnp.zeros((width, width), dtype=gram.dtype)
            for middle in range(outer, inner):
                total = total + jnp.dot(lower_blocks[inner, middle], inverse_blocks[middle, outer], precision=lax.Precision.HIGHEST)
            inverse_blocks[inner, outer] = 0.0 - jnp.dot(inverse_diag[inner], total, precision=lax.Precision.HIGHEST)
    inverse_rows = []
    for inner in range(count):
        inverse_rows.append(jnp.concatenate([inverse_blocks.get((inner, outer), zero_block) for outer in range(count)], 1))
    lower_inverse = jnp.concatenate(inverse_rows, 0)
    return (lower.T, lower_inverse.T)

def tangent(values, viscosity, coupling, offsets):
    padded = jnp.pad(values, ((0, 0), (0, 0), (REACH, REACH)))
    summed = [values[0], values[1], values[2]]
    for which_band in range(BANDS):
        start = (REACH + offsets[which_band]).astype(jnp.int32)
        shifted = lax.dynamic_slice_in_dim(padded, start, CELLS, 2)
        for out_comp in range(3):
            for in_comp in range(3):
                summed[out_comp] = summed[out_comp] + coupling[which_band, out_comp, in_comp][None, :] * shifted[in_comp]
    return viscosity[None, None, :] * jnp.stack(summed)

def adjoint(scaled, coupling, offsets):
    result = scaled
    for which_band in range(BANDS):
        parts = []
        for in_comp in range(3):
            acc = coupling[which_band, 0, in_comp][None, :] * scaled[0]
            acc = acc + coupling[which_band, 1, in_comp][None, :] * scaled[1]
            acc = acc + coupling[which_band, 2, in_comp][None, :] * scaled[2]
            parts.append(acc)
        padded = jnp.pad(jnp.stack(parts), ((0, 0), (0, 0), (REACH, REACH)))
        start = (REACH - offsets[which_band]).astype(jnp.int32)
        result = result + lax.dynamic_slice_in_dim(padded, start, CELLS, 2)
    return result

def hessian(values, viscosity, coupling, weight, offsets):
    image = tangent(values, viscosity, coupling, offsets)
    scaled = viscosity[None, None, :] * (weight[:, None, :] * image)
    return adjoint(scaled, coupling, offsets)

def reference(probes, viscosity, coupling, misfit_weight, band_offsets):
    panel = hessian(probes, viscosity, coupling, misfit_weight, band_offsets)
    panel = hessian(panel, viscosity, coupling, misfit_weight, band_offsets)
    gram = jnp.einsum('kpc,kqc->pq', panel, panel, precision=lax.Precision.HIGHEST) / ROWS
    upper, r_inverse = factorize(gram)
    basis = jnp.einsum('kqc,qp->kpc', panel, r_inverse, precision=lax.Precision.HIGHEST)
    return (basis, upper)
```

```python
import functools

import jax
import jax.numpy as jnp
from jax import lax
from jax.experimental import pallas as pl
from jax.experimental.pallas import tpu as pltpu
from jax.sharding import PartitionSpec as P

REACH = 4
BANDS = 4
HALO = 4 * REACH
TERMS = 9 * BANDS
COEFS = TERMS + 4
TILE = 128
EXACT = lax.Precision.HIGHEST
CLOSE = lax.Precision.HIGH
VMEM = pl.BlockSpec(memory_space=pltpu.VMEM)
PARAMS = pltpu.CompilerParams(vmem_limit_bytes=48 * 2**20)


def pack_kernel(first_ref, last_ref, coef_ref, low_ref, high_ref):
    rows, cells = first_ref.shape[1], coef_ref.shape[1]
    for comp in range(3):
        spot = slice(HALO * comp, HALO * comp + HALO)
        low_ref[spot, :] = first_ref[comp].T[:HALO]
        high_ref[spot, :] = last_ref[comp].T[TILE - HALO :]
    blank = jnp.zeros((rows - COEFS, TILE), jnp.float32)
    spot = slice(3 * HALO, 4 * HALO)
    low_ref[spot, :] = jnp.concatenate([coef_ref[:, :TILE], blank], 0).T[:HALO]
    high_ref[spot, :] = jnp.concatenate([coef_ref[:, cells - TILE :], blank], 0).T[TILE - HALO :]


def pack_edges(probes, coefs):
    _, rows, cells = probes.shape
    edge = jax.ShapeDtypeStruct((4 * HALO, rows), jnp.float32)
    last = cells // TILE - 1
    return pl.pallas_call(
        pack_kernel,
        grid=(1,),
        in_specs=[
            pl.BlockSpec((3, rows, TILE), lambda i: (0, 0, 0)),
            pl.BlockSpec((3, rows, TILE), lambda i: (0, 0, last)),
            pl.BlockSpec((COEFS, cells), lambda i: (0, 0)),
        ],
        out_specs=[pl.BlockSpec((4 * HALO, rows), lambda i: (0, 0))] * 2,
        out_shape=[edge, edge],
        compiler_params=PARAMS,
    )(probes, probes, coefs)


def turned(x, amount):
    if isinstance(amount, int):
        return pltpu.roll(x, (TILE - amount) % TILE, 1)
    return pltpu.roll(x, lax.rem(TILE - amount, TILE), 1)


def moved(tiles, amount, lane):
    turns = [turned(t, amount) for t in tiles]
    return [
        jnp.where(lane < TILE - amount, turns[i], turns[min(i + 1, len(tiles) - 1)])
        for i in range(len(tiles))
    ]


def stretch(own, ends, lane):
    turns = [turned(t, TILE - HALO) for t in own]
    middle = [jnp.where(lane < HALO, turns[i], turns[i + 1]) for i in range(len(own) - 1)]
    return [jnp.where(lane < HALO, ends, turns[0])] + middle + [jnp.where(lane < HALO, turns[-1], ends)]


def panel_kernel(off_ref, x_ref, coef_ref, low_ref, high_ref, out_ref, ends_ref, tab_ref, mid_ref, in_ref):
    _, rows, cells = x_ref.shape
    count = cells // TILE
    lane = lax.broadcasted_iota(jnp.int32, (8, TILE), 1)
    offs = [off_ref[b] for b in range(BANDS)]

    blank = jnp.zeros((TILE - 2 * HALO, rows), jnp.float32)
    for comp in range(4):
        spot = slice(HALO * comp, HALO * comp + HALO)
        ends_ref[comp] = jnp.concatenate([low_ref[spot, :], high_ref[spot, :], blank], 0).T

    for group in range(COEFS // 8):
        spot = slice(8 * group, 8 * group + 8)
        ext = stretch(
            [coef_ref[spot, TILE * i : TILE * i + TILE] for i in range(count)], ends_ref[3, spot, :], lane
        )
        by_step = {(0, b): moved(ext, REACH, lane) for b in range(BANDS)}
        by_step.update({(2, b): moved(ext, 3 * REACH, lane) for b in range(BANDS)})
        for b in range(BANDS):
            by_step[1, b] = moved(ext, 2 * REACH - offs[b], lane)
            by_step[3, b] = moved(ext, 4 * REACH - offs[b], lane)
        for j in range(8):
            row = 8 * group + j
            if row >= TERMS:
                continue
            for step in range(4):
                for i in range(count + 1):
                    tile = by_step[step, row // 9][i]
                    tab_ref[step, row, :, TILE * i : TILE * i + TILE] = jnp.broadcast_to(
                        tile[j : j + 1, :], (8, TILE)
                    )
        if group == COEFS // 8 - 1:
            for half, step in enumerate((0, 2)):
                for i in range(count + 1):
                    tile = by_step[step, 0][i]
                    visc = jnp.broadcast_to(tile[4:5, :], (8, TILE))
                    for comp in range(3):
                        weight = jnp.broadcast_to(tile[5 + comp : 6 + comp, :], (8, TILE))
                        mid_ref[half, comp, :, TILE * i : TILE * i + TILE] = visc * visc * weight
            between = moved(ext, 2 * REACH, lane)
            for at, i in enumerate((0, count)):
                inside = jnp.broadcast_to(between[i][4:5, :], (8, TILE)) != 0.0
                in_ref[at] = jnp.where(inside, 1.0, 0.0)

    masks = {}
    for sign in (1, -1):
        for b in range(BANDS):
            masks[sign, b] = lane < TILE - (REACH + sign * offs[b])
    center = lane < TILE - REACH

    def apply(tiles, step, outs):
        sign = 1 if step % 2 == 0 else -1
        result = [[], [], []]

        def turns_of(i):
            return [
                [turned(tiles[m][i], REACH)]
                + [turned(tiles[m][i], REACH + sign * offs[b]) for b in range(BANDS)]
                for m in range(3)
            ]

        ahead = turns_of(0)
        for i in range(outs):
            here = ahead
            ahead = turns_of(i + 1) if i + 1 < len(tiles[0]) else here
            shifted = [
                [jnp.where(center, here[m][0], ahead[m][0])]
                + [jnp.where(masks[sign, b], here[m][1 + b], ahead[m][1 + b]) for b in range(BANDS)]
                for m in range(3)
            ]
            for k in range(3):
                total = shifted[k][0]
                for b in range(BANDS):
                    for m in range(3):
                        term = 9 * b + (3 * k + m if sign == 1 else 3 * m + k)
                        total = total + tab_ref[step, term, :, TILE * i : TILE * i + TILE] * shifted[m][1 + b]
                if step % 2 == 0:
                    total = total * mid_ref[step // 2, k, :, TILE * i : TILE * i + TILE]
                if step == 1 and i == 0:
                    total = total * in_ref[0]
                if step == 1 and i == count:
                    total = total * in_ref[1]
                result[k].append(total)
        return result

    def group_step(g, carry):
        spot = pl.ds(pl.multiple_of(8 * g, 8), 8)
        tiles = [
            stretch(
                [x_ref[m, spot, TILE * i : TILE * i + TILE] for i in range(count)], ends_ref[m, spot, :], lane
            )
            for m in range(3)
        ]
        for step in range(4):
            tiles = apply(tiles, step, count + 1 if step < 3 else count)
        for m in range(3):
            for i in range(count):
                out_ref[m, spot, TILE * i : TILE * i + TILE] = tiles[m][i]
        return carry

    lax.fori_loop(0, rows // 8, group_step, 0)


def panel_of(probes, coefs, low, high, offsets):
    _, rows, cells = probes.shape
    wide = cells + TILE
    return pl.pallas_call(
        panel_kernel,
        in_specs=[pl.BlockSpec(memory_space=pltpu.SMEM)] + [VMEM] * 4,
        out_specs=VMEM,
        out_shape=jax.ShapeDtypeStruct(probes.shape, jnp.float32),
        scratch_shapes=[
            pltpu.VMEM((4, rows, TILE), jnp.float32),
            pltpu.VMEM((4, TERMS, 8, wide), jnp.float32),
            pltpu.VMEM((2, 3, 8, wide), jnp.float32),
            pltpu.VMEM((2, 8, TILE), jnp.float32),
        ],
        compiler_params=PARAMS,
    )(offsets, probes, coefs, low, high)


def over_lanes(x, j):
    return jnp.broadcast_to(x[:, j : j + 1], (8, TILE))


def over_rows(x, i):
    return jnp.broadcast_to(x[i : i + 1, :], (8, TILE))


def factor_tile(a_ref, e_ref):
    blocks = TILE // 8
    rows = lax.broadcasted_iota(jnp.int32, (8, TILE), 0)
    lanes = lax.broadcasted_iota(jnp.int32, (8, TILE), 1)
    a = [a_ref[8 * t : 8 * t + 8, :] for t in range(blocks)]
    e = [jnp.where(lanes == rows + 8 * t, 1.0, 0.0) for t in range(blocks)]
    below = [rows >= i for i in range(8)]
    for s in range(blocks):
        columns = [over_lanes(a[s], 8 * s + j) for j in range(8)]
        d = {(i, j): over_rows(columns[j], i) for j in range(8) for i in range(j, 8)}
        inv, low = [], {}
        for j in range(8):
            inv.append(lax.rsqrt(d[j, j]))
            for i in range(j + 1, 8):
                low[i, j] = d[i, j] * inv[j]
            for k in range(j + 1, 8):
                for i in range(k, 8):
                    d[i, k] = d[i, k] - low[i, j] * low[k, j]
        w = {}
        for k in range(8):
            w[k, k] = inv[k]
            for i in range(k + 1, 8):
                total = low[i, k] * w[k, k]
                for m in range(k + 1, i):
                    total = total + low[i, m] * w[m, k]
                w[i, k] = -inv[i] * total
        upper = side = None
        for k in range(8):
            mix = jnp.where(below[k], w[k, k], 0.0)
            for i in range(k + 1, 8):
                mix = jnp.where(below[i], w[i, k], mix)
            u, f = mix * over_rows(a[s], k), mix * over_rows(e[s], k)
            upper, side = (u, f) if k == 0 else (upper + u, side + f)
        a[s], e[s] = upper, side
        upper_rows = [over_rows(upper, i) for i in range(8)]
        side_rows = [over_rows(side, i) for i in range(8)]
        for t in range(s + 1, blocks):
            columns = [over_lanes(a[t], 8 * s + j) for j in range(8)]
            for i in range(8):
                factor = w[i, 0] * columns[0]
                for k in range(1, i + 1):
                    factor = factor + w[i, k] * columns[k]
                a[t] = a[t] - factor * upper_rows[i]
                e[t] = e[t] - factor * side_rows[i]
    for t in range(blocks):
        a_ref[8 * t : 8 * t + 8, :] = jnp.where(lanes >= rows + 8 * t, a[t], 0.0)
        e_ref[8 * t : 8 * t + 8, :] = e[t]


def factor_kernel(g_ref, r_ref, x_ref, work, tile_a, tile_e):
    size = g_ref.shape[0]
    dot = functools.partial(jnp.dot, precision=EXACT, preferred_element_type=jnp.float32)

    def outer(left, right):
        return lax.dot_general(
            left, right, (((0,), (0,)), ((), ())), precision=EXACT, preferred_element_type=jnp.float32
        )

    work[...] = g_ref[...]
    rows = lax.broadcasted_iota(jnp.int32, (size, size), 0)
    columns = lax.broadcasted_iota(jnp.int32, (size, size), 1)
    x_ref[...] = jnp.where(rows == columns, 1.0, 0.0)
    lanes = lax.broadcasted_iota(jnp.int32, (TILE, size), 1)

    def block_step(b, carry):
        start = pl.multiple_of(b * TILE, TILE)
        spot = pl.ds(start, TILE)
        tile_a[...] = work[spot, spot]
        factor_tile(tile_a, tile_e)
        inverse = tile_e[...]
        right = jnp.where(lanes >= start + TILE, dot(inverse, work[spot, :]), 0.0)
        side = dot(inverse, x_ref[spot, :])
        r_ref[spot, :] = right
        r_ref[spot, spot] = tile_a[...]
        x_ref[spot, :] = side
        work[...] = work[...] - outer(right, right)
        x_ref[...] = x_ref[...] - outer(right, side)
        return carry

    lax.fori_loop(0, size // TILE, block_step, 0)


def factorize(gram):
    size = gram.shape[0]
    square = jax.ShapeDtypeStruct((size, size), jnp.float32)
    return pl.pallas_call(
        factor_kernel,
        in_specs=[VMEM],
        out_specs=[VMEM, VMEM],
        out_shape=[square, square],
        scratch_shapes=[
            pltpu.VMEM((size, size), jnp.float32),
            pltpu.VMEM((TILE, TILE), jnp.float32),
            pltpu.VMEM((TILE, TILE), jnp.float32),
        ],
        compiler_params=PARAMS,
    )(gram)


def partners(axis, bit):
    return [(i, i ^ bit) for i in range(lax.axis_size(axis))]


def bits_of(axis):
    bits, bit = [], 1
    while bit < lax.axis_size(axis):
        bits.append(bit)
        bit *= 2
    return bits


def scatter_sum(block, axis):
    me = lax.axis_index(axis)
    for bit in bits_of(axis):
        half = block.shape[0] // 2
        upper = (me // bit) % 2
        keep = lax.dynamic_slice_in_dim(block, upper * half, half, 0)
        give = lax.dynamic_slice_in_dim(block, (1 - upper) * half, half, 0)
        block = keep + lax.ppermute(give, axis, partners(axis, bit))
    return block


def gather_back(block, axis, dim):
    me = lax.axis_index(axis)
    for bit in reversed(bits_of(axis)):
        other = lax.ppermute(block, axis, partners(axis, bit))
        upper = (me // bit) % 2 == 1
        block = jnp.concatenate(
            [jnp.where(upper, other, block), jnp.where(upper, block, other)], dim
        )
    return block


def body(probes, viscosity, coupling, misfit_weight, band_offsets):
    _, columns, cells = probes.shape
    slabs, groups = lax.axis_size("slab"), lax.axis_size("probe")
    me = lax.axis_index("probe")
    coefs = jnp.concatenate([coupling.reshape(TERMS, cells), viscosity[None, :], misfit_weight], 0)
    first, last = pack_edges(probes, coefs)
    forward = [(i, i + 1) for i in range(slabs - 1)]
    low = lax.ppermute(last, "slab", forward)
    high = lax.ppermute(first, "slab", [(b, a) for a, b in forward])
    panel = panel_of(probes, coefs, low, high, band_offsets)

    blocks = [panel] + [
        lax.ppermute(panel, "probe", [(i, (i + d) % groups) for i in range(groups)])
        for d in range(1, groups)
    ]
    part = jnp.zeros((groups, columns, columns), jnp.float32)
    for d, block in enumerate(blocks):
        product = jnp.einsum("kpc,kqc->pq", panel, block, precision=CLOSE)
        part = lax.dynamic_update_slice(part, product[None], ((me - d) % groups, 0, 0))
    part = part.transpose(1, 0, 2).reshape(columns, groups * columns) / (3 * cells * slabs)
    share = scatter_sum(part, "slab")
    share = gather_back(share[None], "probe", 0)
    gram = gather_back(share, "slab", 1).reshape(groups * columns, groups * columns)

    upper, inverse = factorize(gram)
    mine = lax.dynamic_slice_in_dim(inverse, me * columns, columns, 0).reshape(columns, groups, columns)
    basis = jnp.zeros_like(panel)
    for d, block in enumerate(blocks):
        mix = lax.dynamic_index_in_dim(mine, (me - d) % groups, 1, keepdims=False)
        basis = basis + jnp.einsum("pq,kqc->kpc", mix, block, precision=CLOSE)
    return basis, lax.dynamic_slice_in_dim(upper, me * columns, columns, 0)


def solution(mesh):
    return jax.shard_map(
        body,
        mesh=mesh,
        in_specs=(
            P(None, "probe", "slab"),
            P("slab"),
            P(None, None, None, "slab"),
            P(None, "slab"),
            P(),
        ),
        out_specs=(P(None, "probe", "slab"), P("probe", None)),
        check_vma=False,
    )
```

```python
import functools

import jax
import jax.numpy as jnp
from jax import lax
from jax.experimental import pallas as pl
from jax.experimental.pallas import tpu as pltpu
from jax.sharding import PartitionSpec as P

REACH = 4
BANDS = 4
HALO = 4 * REACH
TERMS = 9 * BANDS
COEFS = TERMS + 4
TILE = 128
EXACT = lax.Precision.HIGHEST
CLOSE = lax.Precision.HIGH
VMEM = pl.BlockSpec(memory_space=pltpu.VMEM)
PARAMS = pltpu.CompilerParams(vmem_limit_bytes=48 * 2**20)


def pack_kernel(first_ref, before_ref, after_ref, last_ref, coef_ref, low_ref, mid_ref, high_ref):
    rows, cells = first_ref.shape[1], coef_ref.shape[1]
    blank = jnp.zeros((rows - COEFS, TILE), jnp.float32)

    def pack(out_ref, x_ref, start, spot):
        for comp in range(3):
            out_ref[HALO * comp : HALO * comp + HALO, :] = x_ref[comp].T[spot]
        coef = jnp.concatenate([coef_ref[:, start : start + TILE], blank], 0)
        out_ref[3 * HALO : 4 * HALO, :] = coef.T[spot]

    head, tail = slice(0, HALO), slice(TILE - HALO, TILE)
    pack(low_ref, first_ref, 0, head)
    pack(high_ref, last_ref, cells - TILE, tail)
    is_first = lax.axis_index("probe") == 0

    @pl.when(is_first)
    def _():
        pack(mid_ref, after_ref, cells // 2, head)

    @pl.when(jnp.logical_not(is_first))
    def _():
        pack(mid_ref, before_ref, cells // 2 - TILE, tail)


def pack_edges(probes, coefs):
    _, rows, cells = probes.shape
    edge = jax.ShapeDtypeStruct((4 * HALO, rows), jnp.float32)
    half = cells // TILE // 2

    def tile(at):
        return pl.BlockSpec((3, rows, TILE), lambda i: (0, 0, at))

    return pl.pallas_call(
        pack_kernel,
        grid=(1,),
        in_specs=[tile(0), tile(half - 1), tile(half), tile(2 * half - 1)]
        + [pl.BlockSpec((COEFS, cells), lambda i: (0, 0))],
        out_specs=[pl.BlockSpec((4 * HALO, rows), lambda i: (0, 0))] * 3,
        out_shape=[edge] * 3,
        compiler_params=PARAMS,
    )(probes, probes, probes, probes, coefs)


def turned(x, amount):
    if isinstance(amount, int):
        return pltpu.roll(x, (TILE - amount) % TILE, 1)
    return pltpu.roll(x, lax.rem(TILE - amount, TILE), 1)


def moved(tiles, amount, lane):
    turns = [turned(t, amount) for t in tiles]
    return [
        jnp.where(lane < TILE - amount, turns[i], turns[min(i + 1, len(tiles) - 1)])
        for i in range(len(tiles))
    ]


def stretch(own, ends, lane):
    turns = [turned(t, TILE - HALO) for t in own]
    middle = [jnp.where(lane < HALO, turns[i], turns[i + 1]) for i in range(len(own) - 1)]
    return [jnp.where(lane < HALO, ends, turns[0])] + middle + [jnp.where(lane < HALO, turns[-1], ends)]


def panel_steps(off_ref, x_ref, coef_ref, low_ref, high_ref, out_refs, ends_ref, tab_ref, mid_ref, in_ref):
    _, rows, cells = x_ref.shape
    share = cells // TILE // len(out_refs)
    count = cells // TILE
    lane = lax.broadcasted_iota(jnp.int32, (8, TILE), 1)
    offs = [off_ref[b] for b in range(BANDS)]

    blank = jnp.zeros((TILE - 2 * HALO, rows), jnp.float32)
    for comp in range(4):
        spot = slice(HALO * comp, HALO * comp + HALO)
        ends_ref[comp] = jnp.concatenate([low_ref[spot, :], high_ref[spot, :], blank], 0).T

    for group in range(COEFS // 8):
        spot = slice(8 * group, 8 * group + 8)
        ext = stretch(
            [coef_ref[spot, TILE * i : TILE * i + TILE] for i in range(count)], ends_ref[3, spot, :], lane
        )
        by_step = {(0, b): moved(ext, REACH, lane) for b in range(BANDS)}
        by_step.update({(2, b): moved(ext, 3 * REACH, lane) for b in range(BANDS)})
        for b in range(BANDS):
            by_step[1, b] = moved(ext, 2 * REACH - offs[b], lane)
            by_step[3, b] = moved(ext, 4 * REACH - offs[b], lane)
        for j in range(8):
            row = 8 * group + j
            if row >= TERMS:
                continue
            for step in range(4):
                for i in range(count + 1):
                    tile = by_step[step, row // 9][i]
                    tab_ref[step, row, :, TILE * i : TILE * i + TILE] = jnp.broadcast_to(
                        tile[j : j + 1, :], (8, TILE)
                    )
        if group == COEFS // 8 - 1:
            for half, step in enumerate((0, 2)):
                for i in range(count + 1):
                    tile = by_step[step, 0][i]
                    visc = jnp.broadcast_to(tile[4:5, :], (8, TILE))
                    for comp in range(3):
                        weight = jnp.broadcast_to(tile[5 + comp : 6 + comp, :], (8, TILE))
                        mid_ref[half, comp, :, TILE * i : TILE * i + TILE] = visc * visc * weight
            between = moved(ext, 2 * REACH, lane)
            for at, i in enumerate((0, count)):
                inside = jnp.broadcast_to(between[i][4:5, :], (8, TILE)) != 0.0
                in_ref[at] = jnp.where(inside, 1.0, 0.0)

    masks = {}
    for sign in (1, -1):
        for b in range(BANDS):
            masks[sign, b] = lane < TILE - (REACH + sign * offs[b])
    center = lane < TILE - REACH

    def apply(tiles, step, outs):
        sign = 1 if step % 2 == 0 else -1
        result = [[], [], []]

        def turns_of(i):
            return [
                [turned(tiles[m][i], REACH)]
                + [turned(tiles[m][i], REACH + sign * offs[b]) for b in range(BANDS)]
                for m in range(3)
            ]

        ahead = turns_of(0)
        for i in range(outs):
            here = ahead
            ahead = turns_of(i + 1) if i + 1 < len(tiles[0]) else here
            shifted = [
                [jnp.where(center, here[m][0], ahead[m][0])]
                + [jnp.where(masks[sign, b], here[m][1 + b], ahead[m][1 + b]) for b in range(BANDS)]
                for m in range(3)
            ]
            for k in range(3):
                total = shifted[k][0]
                for b in range(BANDS):
                    for m in range(3):
                        term = 9 * b + (3 * k + m if sign == 1 else 3 * m + k)
                        total = total + tab_ref[step, term, :, TILE * i : TILE * i + TILE] * shifted[m][1 + b]
                if step % 2 == 0:
                    total = total * mid_ref[step // 2, k, :, TILE * i : TILE * i + TILE]
                if step == 1 and i == 0:
                    total = total * in_ref[0]
                if step == 1 and i == count:
                    total = total * in_ref[1]
                result[k].append(total)
        return result

    def group_step(g, carry):
        spot = pl.ds(pl.multiple_of(8 * g, 8), 8)
        tiles = [
            stretch(
                [x_ref[m, spot, TILE * i : TILE * i + TILE] for i in range(count)], ends_ref[m, spot, :], lane
            )
            for m in range(3)
        ]
        for step in range(4):
            tiles = apply(tiles, step, count + 1 if step < 3 else count)
        for m in range(3):
            for i in range(count):
                out_refs[i // share][m, spot, pl.ds(TILE * (i % share), TILE)] = tiles[m][i]
        return carry

    lax.fori_loop(0, rows // 8, group_step, 0)


def panel_scratch(rows, cells):
    wide = cells + TILE
    return [
        pltpu.VMEM((4, rows, TILE), jnp.float32),
        pltpu.VMEM((4, TERMS, 8, wide), jnp.float32),
        pltpu.VMEM((2, 3, 8, wide), jnp.float32),
        pltpu.VMEM((2, 8, TILE), jnp.float32),
    ]


SMEM = pl.BlockSpec(memory_space=pltpu.SMEM)


def pieces(x):
    high = x.astype(jnp.bfloat16)
    return high, (x - high.astype(jnp.float32)).astype(jnp.bfloat16)


def close_dot(left, right, over):
    dot = functools.partial(lax.dot_general, dimension_numbers=((over, ((), ()))), preferred_element_type=jnp.float32)
    return dot(left[0], right[0]) + (dot(left[0], right[1]) + dot(left[1], right[0]))


ALONG = ((1,), (1,))
PLAIN = ((1,), (0,))


def own_kernel(scale, *refs):
    *ins, first_ref, second_ref, gram_ref = refs[:8]
    panel_steps(*ins, (first_ref, second_ref), *refs[8:])
    total = None
    for ref in (first_ref, second_ref):
        for k in range(3):
            x = pieces(ref[k])
            part = close_dot(x, x, ALONG)
            total = part if total is None else total + part
    gram_ref[...] = total * scale


def panel_of(probes, coefs, low, high, offsets, scale):
    _, rows, cells = probes.shape
    half = jax.ShapeDtypeStruct((3, rows, cells // 2), jnp.float32)
    return pl.pallas_call(
        functools.partial(own_kernel, scale),
        in_specs=[SMEM] + [VMEM] * 4,
        out_specs=[VMEM] * 3,
        out_shape=[half, half, jax.ShapeDtypeStruct((rows, rows), jnp.float32)],
        scratch_shapes=panel_scratch(rows, cells),
        compiler_params=PARAMS,
    )(offsets, probes, coefs, low, high)


def reversed_bits(place, count):
    result, bit = 0, 1
    while bit < count:
        result = 2 * result + (place // bit) % 2
        bit *= 2
    return result


def block_at(place, count):
    return lax.bitwise_xor(lax.axis_index("slab"), jnp.int32(reversed_bits(place, count)))


def cross_kernel(scale, count, *refs):
    *ins, first_ref, second_ref, gram_ref, other_ref, out_ref = refs[:10]
    panel_steps(*ins, (other_ref,), *refs[10:-1])
    work = refs[-1]
    rows = gram_ref.shape[0]
    is_first = lax.axis_index("probe") == 0

    def product(left, right):
        total = None
        for k in range(3):
            part = close_dot(pieces(left[k]), pieces(right[k]), ALONG)
            total = part if total is None else total + part
        work[...] = total * scale

    @pl.when(is_first)
    def _():
        product(second_ref, other_ref)

    @pl.when(jnp.logical_not(is_first))
    def _():
        product(other_ref, first_ref)

    share = rows // count
    for place in range(count):
        spot = pl.ds(pl.multiple_of(block_at(place, count) * share, share), share)
        out_ref[share * place : share * place + share, :rows] = gram_ref[spot, :]
        out_ref[share * place : share * place + share, rows:] = work[spot, :]


def cross_of(half, coefs, low, high, offsets, first, second, gram, scale, count):
    _, rows, cells = half.shape
    return pl.pallas_call(
        functools.partial(cross_kernel, scale, count),
        in_specs=[SMEM] + [VMEM] * 7,
        out_specs=[VMEM] * 2,
        out_shape=[
            jax.ShapeDtypeStruct(half.shape, jnp.float32),
            jax.ShapeDtypeStruct((rows, 2 * rows), jnp.float32),
        ],
        scratch_shapes=panel_scratch(rows, cells) + [pltpu.VMEM((rows, rows), jnp.float32)],
        compiler_params=PARAMS,
    )(offsets, half, coefs, low, high, first, second, gram)


def over_lanes(x, j):
    return jnp.broadcast_to(x[:, j : j + 1], (8, TILE))


def over_rows(x, i):
    return jnp.broadcast_to(x[i : i + 1, :], (8, TILE))


def factor_tile(a_ref, e_ref):
    blocks = TILE // 8
    rows = lax.broadcasted_iota(jnp.int32, (8, TILE), 0)
    lanes = lax.broadcasted_iota(jnp.int32, (8, TILE), 1)
    a = [a_ref[8 * t : 8 * t + 8, :] for t in range(blocks)]
    e = [jnp.where(lanes == rows + 8 * t, 1.0, 0.0) for t in range(blocks)]
    below = [rows >= i for i in range(8)]
    for s in range(blocks):
        columns = [over_lanes(a[s], 8 * s + j) for j in range(8)]
        d = {(i, j): over_rows(columns[j], i) for j in range(8) for i in range(j, 8)}
        inv, low = [], {}
        for j in range(8):
            inv.append(lax.rsqrt(d[j, j]))
            for i in range(j + 1, 8):
                low[i, j] = d[i, j] * inv[j]
            for k in range(j + 1, 8):
                for i in range(k, 8):
                    d[i, k] = d[i, k] - low[i, j] * low[k, j]
        w = {}
        for k in range(8):
            w[k, k] = inv[k]
            for i in range(k + 1, 8):
                total = low[i, k] * w[k, k]
                for m in range(k + 1, i):
                    total = total + low[i, m] * w[m, k]
                w[i, k] = -inv[i] * total
        upper = side = None
        for k in range(8):
            mix = jnp.where(below[k], w[k, k], 0.0)
            for i in range(k + 1, 8):
                mix = jnp.where(below[i], w[i, k], mix)
            u, f = mix * over_rows(a[s], k), mix * over_rows(e[s], k)
            upper, side = (u, f) if k == 0 else (upper + u, side + f)
        a[s], e[s] = upper, side
        upper_rows = [over_rows(upper, i) for i in range(8)]
        side_rows = [over_rows(side, i) for i in range(8)]
        for t in range(s + 1, blocks):
            columns = [over_lanes(a[t], 8 * s + j) for j in range(8)]
            for i in range(8):
                factor = w[i, 0] * columns[0]
                for k in range(1, i + 1):
                    factor = factor + w[i, k] * columns[k]
                a[t] = a[t] - factor * upper_rows[i]
                e[t] = e[t] - factor * side_rows[i]
    for t in range(blocks):
        a_ref[8 * t : 8 * t + 8, :] = jnp.where(lanes >= rows + 8 * t, a[t], 0.0)
        e_ref[8 * t : 8 * t + 8, :] = e[t]


def factor_steps(work, r_ref, x_ref, tile_a, tile_e):
    size = work.shape[0]
    dot = functools.partial(jnp.dot, precision=EXACT, preferred_element_type=jnp.float32)

    def outer(left, right):
        return lax.dot_general(
            left, right, (((0,), (0,)), ((), ())), precision=EXACT, preferred_element_type=jnp.float32
        )

    rows = lax.broadcasted_iota(jnp.int32, (size, size), 0)
    columns = lax.broadcasted_iota(jnp.int32, (size, size), 1)
    x_ref[...] = jnp.where(rows == columns, 1.0, 0.0)
    lanes = lax.broadcasted_iota(jnp.int32, (TILE, size), 1)

    def block_step(b, carry):
        start = pl.multiple_of(b * TILE, TILE)
        spot = pl.ds(start, TILE)
        tile_a[...] = work[spot, spot]
        factor_tile(tile_a, tile_e)
        inverse = tile_e[...]
        right = jnp.where(lanes >= start + TILE, dot(inverse, work[spot, :]), 0.0)
        side = dot(inverse, x_ref[spot, :])
        r_ref[spot, :] = right
        r_ref[spot, spot] = tile_a[...]
        x_ref[spot, :] = side
        work[...] = work[...] - outer(right, right)
        x_ref[...] = x_ref[...] - outer(right, side)
        return carry

    lax.fori_loop(0, size // TILE, block_step, 0)


def factor_scratch(size):
    return [pltpu.VMEM((size, size), jnp.float32)] + [pltpu.VMEM((TILE, TILE), jnp.float32)] * 2


def factor_kernel(g_ref, r_ref, x_ref, work, tile_a, tile_e):
    work[...] = g_ref[...]
    factor_steps(work, r_ref, x_ref, tile_a, tile_e)


def factorize(gram):
    size = gram.shape[0]
    square = jax.ShapeDtypeStruct((size, size), jnp.float32)
    return pl.pallas_call(
        factor_kernel,
        in_specs=[VMEM],
        out_specs=[VMEM, VMEM],
        out_shape=[square, square],
        scratch_shapes=factor_scratch(size),
        compiler_params=PARAMS,
    )(gram)


def pair_kernel(count, g_ref, r_ref, own_ref, other_ref, work, tile_a, tile_e, r_all, x_all):
    rows = r_ref.shape[0]
    share = rows // count
    work[rows:, :rows] = jnp.zeros((rows, rows), jnp.float32)
    for place in range(count):
        start = pl.multiple_of(block_at(place, count) * share, share)
        here = slice(share * place, share * place + share)
        work[pl.ds(start, share), :] = g_ref[here, : 2 * rows]
        work[pl.ds(rows + start, share), rows:] = g_ref[here, 2 * rows :]
    factor_steps(work, r_all, x_all, tile_a, tile_e)
    is_first = lax.axis_index("probe") == 0

    @pl.when(is_first)
    def _():
        r_ref[...] = r_all[:rows, :]
        own_ref[...] = x_all[:rows, :rows]
        other_ref[...] = jnp.zeros((rows, rows), jnp.float32)

    @pl.when(jnp.logical_not(is_first))
    def _():
        r_ref[...] = r_all[rows:, :]
        own_ref[...] = x_all[rows:, rows:]
        other_ref[...] = x_all[rows:, :rows]


def factorize_pair(travelled, count):
    rows = travelled.shape[0]
    square = jax.ShapeDtypeStruct((rows, rows), jnp.float32)
    return pl.pallas_call(
        functools.partial(pair_kernel, count),
        in_specs=[VMEM],
        out_specs=[VMEM] * 3,
        out_shape=[jax.ShapeDtypeStruct((rows, 2 * rows), jnp.float32), square, square],
        scratch_shapes=factor_scratch(2 * rows) + [pltpu.VMEM((2 * rows, 2 * rows), jnp.float32)] * 2,
        compiler_params=PARAMS,
    )(travelled)


def basis_kernel(own_ref, other_ref, first_ref, second_ref, front_ref, back_ref, out_ref):
    half = first_ref.shape[2]
    own, other = pieces(own_ref[...]), pieces(other_ref[...])
    for at, (mine, theirs) in enumerate(((first_ref, front_ref), (second_ref, back_ref))):
        out_ref[0, :, half * at : half * at + half] = close_dot(own, pieces(mine[0]), PLAIN) + close_dot(
            other, pieces(theirs[0]), PLAIN
        )


def basis_of(own, other, first, second, front, back):
    _, rows, half = first.shape
    weights = pl.BlockSpec((rows, rows), lambda k: (0, 0))
    panel = pl.BlockSpec((1, rows, half), lambda k: (k, 0, 0))
    return pl.pallas_call(
        basis_kernel,
        grid=(3,),
        in_specs=[weights] * 2 + [panel] * 4,
        out_specs=pl.BlockSpec((1, rows, 2 * half), lambda k: (k, 0, 0)),
        out_shape=jax.ShapeDtypeStruct((3, rows, 2 * half), jnp.float32),
        compiler_params=PARAMS,
    )(own, other, first, second, front, back)


def partners(axis, bit):
    return [(i, i ^ bit) for i in range(lax.axis_size(axis))]


def bits_of(axis):
    bits, bit = [], 1
    while bit < lax.axis_size(axis):
        bits.append(bit)
        bit *= 2
    return bits


def scatter_sum(block, axis):
    for bit in bits_of(axis):
        half = block.shape[0] // 2
        block = block[:half] + lax.ppermute(block[half:], axis, partners(axis, bit))
    return block


def gather_back(block, axis):
    for bit in reversed(bits_of(axis)):
        block = jnp.concatenate([block, lax.ppermute(block, axis, partners(axis, bit))], 0)
    return block


def swapped(block):
    return lax.ppermute(block, "probe", [(0, 1), (1, 0)])


def pair_body(probes, coefs, offsets):
    _, columns, cells = probes.shape
    slabs = lax.axis_size("slab")
    scale = 1.0 / (3 * cells * slabs)
    is_first = lax.axis_index("probe") == 0
    half = cells // 2
    theirs = swapped(jnp.where(is_first, probes[:, :, :half], probes[:, :, half:]))
    first, mid, last = pack_edges(probes, coefs)
    forward = [(i, i + 1) for i in range(slabs - 1)]
    low = lax.ppermute(last, "slab", forward)
    high = lax.ppermute(first, "slab", [(b, a) for a, b in forward])
    ends = swapped(jnp.where(is_first, jnp.concatenate([low, mid], 0), jnp.concatenate([mid, high], 0)))
    front, back, gram = panel_of(probes, coefs, low, high, offsets, scale)
    their_back = lax.ppermute(back, "probe", [(0, 1)])
    half_coefs = jnp.where(is_first, coefs[:, half:], coefs[:, :half])
    their_front, sums = cross_of(
        theirs, half_coefs, ends[: 4 * HALO], ends[4 * HALO :], offsets, front, back, gram, scale, slabs
    )
    share = scatter_sum(sums, "slab")
    other = swapped(share)
    share = jnp.concatenate(
        [
            jnp.where(is_first, share[:, :columns], other[:, :columns]),
            share[:, columns:] + other[:, columns:],
            jnp.where(is_first, other[:, :columns], share[:, :columns]),
        ],
        1,
    )
    r_rows, own, other = factorize_pair(gather_back(share, "slab"), slabs)
    return basis_of(own, other, front, back, their_front, their_back), r_rows


def whole_body(probes, coefs, offsets):
    _, columns, cells = probes.shape
    slabs, groups = lax.axis_size("slab"), lax.axis_size("probe")
    me = lax.axis_index("probe")
    scale = 1.0 / (3 * cells * slabs)
    first, _, last = pack_edges(probes, coefs)
    forward = [(i, i + 1) for i in range(slabs - 1)]
    low = lax.ppermute(last, "slab", forward)
    high = lax.ppermute(first, "slab", [(b, a) for a, b in forward])
    front, back, _ = panel_of(probes, coefs, low, high, offsets, scale)
    panel = jnp.concatenate([front, back], 2)
    everyone = lax.all_gather(panel, "probe", axis=1, tiled=True)
    part = scale * jnp.einsum("kpc,kqc->pq", panel, everyone, precision=CLOSE)
    gram = lax.all_gather(lax.psum(part, "slab"), "probe", axis=0, tiled=True)
    upper, inverse = factorize(gram)
    mine = lax.dynamic_slice_in_dim(inverse, me * columns, columns, 0)
    basis = jnp.einsum("pq,kqc->kpc", mine, everyone, precision=CLOSE)
    return basis, lax.dynamic_slice_in_dim(upper, me * columns, columns, 0)


def body(probes, viscosity, coupling, misfit_weight, band_offsets):
    coefs = jnp.concatenate([coupling.reshape(TERMS, -1), viscosity[None, :], misfit_weight], 0)
    run = pair_body if lax.axis_size("probe") == 2 else whole_body
    return run(probes, coefs, band_offsets)


def solution(mesh):
    return jax.shard_map(
        body,
        mesh=mesh,
        in_specs=(
            P(None, "probe", "slab"),
            P("slab"),
            P(None, None, None, "slab"),
            P(None, "slab"),
            P(),
        ),
        out_specs=(P(None, "probe", "slab"), P("probe", None)),
        check_vma=False,
    )
```

```python
import functools

import jax
import jax.numpy as jnp
from jax import lax
from jax.experimental import pallas as pl
from jax.experimental.pallas import tpu as pltpu
from jax.sharding import PartitionSpec as P

REACH = 4
BANDS = 4
HALO = 4 * REACH
TERMS = 9 * BANDS
COEFS = TERMS + 4
TILE = 128
EARLY = 1
AT_ONCE = 4
EXACT = lax.Precision.HIGHEST
CLOSE = lax.Precision.HIGH
VMEM = pl.BlockSpec(memory_space=pltpu.VMEM)
PARAMS = pltpu.CompilerParams(vmem_limit_bytes=48 * 2**20)


def pack_kernel(first_ref, before_ref, after_ref, last_ref, coef_ref, low_ref, mid_ref, high_ref):
    rows, cells = first_ref.shape[1], coef_ref.shape[1]
    blank = jnp.zeros((rows - COEFS, TILE), jnp.float32)

    def pack(out_ref, x_ref, start, spot):
        for comp in range(3):
            out_ref[HALO * comp : HALO * comp + HALO, :] = x_ref[comp].T[spot]
        coef = jnp.concatenate([coef_ref[:, start : start + TILE], blank], 0)
        out_ref[3 * HALO : 4 * HALO, :] = coef.T[spot]

    head, tail = slice(0, HALO), slice(TILE - HALO, TILE)
    pack(low_ref, first_ref, 0, head)
    pack(high_ref, last_ref, cells - TILE, tail)
    is_first = lax.axis_index("probe") == 0

    @pl.when(is_first)
    def _():
        pack(mid_ref, after_ref, cells // 2, head)

    @pl.when(jnp.logical_not(is_first))
    def _():
        pack(mid_ref, before_ref, cells // 2 - TILE, tail)


def pack_edges(probes, coefs):
    _, rows, cells = probes.shape
    edge = jax.ShapeDtypeStruct((4 * HALO, rows), jnp.float32)
    half = cells // TILE // 2

    def tile(at):
        return pl.BlockSpec((3, rows, TILE), lambda i: (0, 0, at))

    return pl.pallas_call(
        pack_kernel,
        grid=(1,),
        in_specs=[tile(0), tile(half - 1), tile(half), tile(2 * half - 1)]
        + [pl.BlockSpec((COEFS, cells), lambda i: (0, 0))],
        out_specs=[pl.BlockSpec((4 * HALO, rows), lambda i: (0, 0))] * 3,
        out_shape=[edge] * 3,
        compiler_params=PARAMS,
    )(probes, probes, probes, probes, coefs)


def turned(x, amount):
    if isinstance(amount, int):
        return pltpu.roll(x, (TILE - amount) % TILE, 1)
    return pltpu.roll(x, lax.rem(TILE - amount, TILE), 1)


def moved(tiles, amount, lane):
    turns = [turned(t, amount) for t in tiles]
    return [
        jnp.where(lane < TILE - amount, turns[i], turns[min(i + 1, len(tiles) - 1)])
        for i in range(len(tiles))
    ]


def stretch(own, ends, lane):
    turns = [turned(t, TILE - HALO) for t in own]
    middle = [jnp.where(lane < HALO, turns[i], turns[i + 1]) for i in range(len(own) - 1)]
    return [jnp.where(lane < HALO, ends, turns[0])] + middle + [jnp.where(lane < HALO, turns[-1], ends)]


def panel_steps(off_ref, x_ref, coef_ref, low_ref, high_ref, out_refs, ends_ref, tab_ref, mid_ref, in_ref):
    _, rows, cells = x_ref.shape
    share = cells // TILE // len(out_refs)
    count = cells // TILE
    lane = lax.broadcasted_iota(jnp.int32, (8, TILE), 1)
    offs = [off_ref[b] for b in range(BANDS)]

    blank = jnp.zeros((TILE - 2 * HALO, rows), jnp.float32)
    for comp in range(4):
        spot = slice(HALO * comp, HALO * comp + HALO)
        ends_ref[comp] = jnp.concatenate([low_ref[spot, :], high_ref[spot, :], blank], 0).T

    for group in range(COEFS // 8):
        spot = slice(8 * group, 8 * group + 8)
        ext = stretch(
            [coef_ref[spot, TILE * i : TILE * i + TILE] for i in range(count)], ends_ref[3, spot, :], lane
        )
        by_step = {(0, b): moved(ext, REACH, lane) for b in range(BANDS)}
        by_step.update({(2, b): moved(ext, 3 * REACH, lane) for b in range(BANDS)})
        for b in range(BANDS):
            by_step[1, b] = moved(ext, 2 * REACH - offs[b], lane)
            by_step[3, b] = moved(ext, 4 * REACH - offs[b], lane)
        for j in range(8):
            row = 8 * group + j
            if row >= TERMS:
                continue
            for step in range(4):
                for i in range(count + 1):
                    tile = by_step[step, row // 9][i]
                    tab_ref[step, row, :, TILE * i : TILE * i + TILE] = jnp.broadcast_to(
                        tile[j : j + 1, :], (8, TILE)
                    )
        if group == COEFS // 8 - 1:
            for half, step in enumerate((0, 2)):
                for i in range(count + 1):
                    tile = by_step[step, 0][i]
                    visc = jnp.broadcast_to(tile[4:5, :], (8, TILE))
                    for comp in range(3):
                        weight = jnp.broadcast_to(tile[5 + comp : 6 + comp, :], (8, TILE))
                        mid_ref[half, comp, :, TILE * i : TILE * i + TILE] = visc * visc * weight
            between = moved(ext, 2 * REACH, lane)
            for at, i in enumerate((0, count)):
                inside = jnp.broadcast_to(between[i][4:5, :], (8, TILE)) != 0.0
                in_ref[at] = jnp.where(inside, 1.0, 0.0)

    masks = {}
    for sign in (1, -1):
        for b in range(BANDS):
            masks[sign, b] = lane < TILE - (REACH + sign * offs[b])
    center = lane < TILE - REACH

    def apply(tiles, step, outs):
        sign = 1 if step % 2 == 0 else -1
        result = [[[], [], []] for _ in range(AT_ONCE)]

        def turns_of(i):
            return [
                [
                    [turned(row[i], REACH)] + [turned(row[i], REACH + sign * offs[b]) for b in range(BANDS)]
                    for row in tiles[at]
                ]
                for at in range(AT_ONCE)
            ]

        ahead = turns_of(0)
        for i in range(outs):
            here = ahead
            ahead = turns_of(i + 1) if i + 1 < len(tiles[0][0]) else here
            spot = slice(TILE * i, TILE * i + TILE)
            shifted = [
                [
                    [jnp.where(center, here[at][m][0], ahead[at][m][0])]
                    + [
                        jnp.where(masks[sign, b], here[at][m][1 + b], ahead[at][m][1 + b])
                        for b in range(BANDS)
                    ]
                    for m in range(3)
                ]
                for at in range(AT_ONCE)
            ]

            def sums(k):
                total = [shifted[at][k][0] for at in range(AT_ONCE)]
                for b in range(BANDS):
                    for m in range(3):
                        term = 9 * b + (3 * k + m if sign == 1 else 3 * m + k)
                        table = tab_ref[step, term, :, spot]
                        total = [total[at] + table * shifted[at][m][1 + b] for at in range(AT_ONCE)]
                return total

            for k in range(3):
                total = sums(k)
                if step % 2 == 0:
                    middle = mid_ref[step // 2, k, :, spot]
                    total = [x * middle for x in total]
                if step == 1 and i in (0, count):
                    inside = in_ref[0 if i == 0 else 1]
                    total = [x * inside for x in total]
                for at in range(AT_ONCE):
                    result[at][k].append(total[at])
        return result

    def group_step(g, carry):
        spots = [pl.ds(pl.multiple_of(8 * (AT_ONCE * g + at), 8), 8) for at in range(AT_ONCE)]
        tiles = [
            [
                stretch(
                    [x_ref[m, spot, TILE * i : TILE * i + TILE] for i in range(count)], ends_ref[m, spot, :], lane
                )
                for m in range(3)
            ]
            for spot in spots
        ]
        for step in range(4):
            tiles = apply(tiles, step, count + 1 if step < 3 else count)
        for at, spot in enumerate(spots):
            for m in range(3):
                for i in range(count):
                    out_refs[i // share][m, spot, pl.ds(TILE * (i % share), TILE)] = tiles[at][m][i]
        return carry

    lax.fori_loop(0, rows // (8 * AT_ONCE), group_step, 0)


def panel_scratch(rows, cells):
    wide = cells + TILE
    return [
        pltpu.VMEM((4, rows, TILE), jnp.float32),
        pltpu.VMEM((4, TERMS, 8, wide), jnp.float32),
        pltpu.VMEM((2, 3, 8, wide), jnp.float32),
        pltpu.VMEM((2, 8, TILE), jnp.float32),
    ]


SMEM = pl.BlockSpec(memory_space=pltpu.SMEM)


def pieces(x):
    high = x.astype(jnp.bfloat16)
    return high, (x - high.astype(jnp.float32)).astype(jnp.bfloat16)


def close_dot(left, right, over):
    dot = functools.partial(lax.dot_general, dimension_numbers=((over, ((), ()))), preferred_element_type=jnp.float32)
    return dot(left[0], right[0]) + (dot(left[0], right[1]) + dot(left[1], right[0]))


ALONG = ((1,), (1,))
PLAIN = ((1,), (0,))
ACROSS = ((0,), (0,))


def own_kernel(scale, *refs):
    *ins, first_ref, second_ref, gram_ref = refs[:8]
    panel_steps(*ins, (first_ref, second_ref), *refs[8:])
    total = None
    for ref in (first_ref, second_ref):
        for k in range(3):
            x = pieces(ref[k])
            part = close_dot(x, x, ALONG)
            total = part if total is None else total + part
    gram_ref[...] = total * scale


def panel_of(probes, coefs, low, high, offsets, scale):
    _, rows, cells = probes.shape
    half = jax.ShapeDtypeStruct((3, rows, cells // 2), jnp.float32)
    return pl.pallas_call(
        functools.partial(own_kernel, scale),
        in_specs=[SMEM] + [VMEM] * 4,
        out_specs=[VMEM] * 3,
        out_shape=[half, half, jax.ShapeDtypeStruct((rows, rows), jnp.float32)],
        scratch_shapes=panel_scratch(rows, cells),
        compiler_params=PARAMS,
    )(offsets, probes, coefs, low, high)


def reversed_bits(place, count):
    result, bit = 0, 1
    while bit < count:
        result = 2 * result + (place // bit) % 2
        bit *= 2
    return result


def block_at(place, count):
    return lax.bitwise_xor(lax.axis_index("slab"), jnp.int32(reversed_bits(place, count)))


def cross_kernel(scale, count, *refs):
    *ins, first_ref, second_ref, gram_ref, other_ref, out_ref = refs[:10]
    panel_steps(*ins, (other_ref,), *refs[10:-1])
    work = refs[-1]
    rows = gram_ref.shape[0]
    is_first = lax.axis_index("probe") == 0

    def product(left, right):
        total = None
        for k in range(3):
            part = close_dot(pieces(left[k]), pieces(right[k]), ALONG)
            total = part if total is None else total + part
        work[...] = total * scale

    @pl.when(is_first)
    def _():
        product(second_ref, other_ref)

    @pl.when(jnp.logical_not(is_first))
    def _():
        product(other_ref, first_ref)

    share = rows // count
    for place in range(count):
        spot = pl.ds(pl.multiple_of(block_at(place, count) * share, share), share)
        out_ref[share * place : share * place + share, :rows] = gram_ref[spot, :]
        out_ref[share * place : share * place + share, rows:] = work[spot, :]


def cross_of(half, coefs, low, high, offsets, first, second, gram, scale, count):
    _, rows, cells = half.shape
    return pl.pallas_call(
        functools.partial(cross_kernel, scale, count),
        in_specs=[SMEM] + [VMEM] * 7,
        out_specs=[VMEM] * 2,
        out_shape=[
            jax.ShapeDtypeStruct(half.shape, jnp.float32),
            jax.ShapeDtypeStruct((rows, 2 * rows), jnp.float32),
        ],
        scratch_shapes=panel_scratch(rows, cells) + [pltpu.VMEM((rows, rows), jnp.float32)],
        compiler_params=PARAMS,
    )(offsets, half, coefs, low, high, first, second, gram)


def over_lanes(x, j):
    return jnp.broadcast_to(x[:, j : j + 1], (8, TILE))


def over_rows(x, i):
    return jnp.broadcast_to(x[i : i + 1, :], (8, TILE))


def factor_tile(a_ref, e_ref):
    blocks = TILE // 8
    rows = lax.broadcasted_iota(jnp.int32, (8, TILE), 0)
    lanes = lax.broadcasted_iota(jnp.int32, (8, TILE), 1)
    a = [a_ref[8 * t : 8 * t + 8, :] for t in range(blocks)]
    e = [jnp.where(lanes == rows + 8 * t, 1.0, 0.0) for t in range(blocks)]

    def repeated(t, s):
        return [over_lanes(a[t], 8 * s + j) for j in range(8)]

    ready = {}
    for s in range(blocks):
        columns = {t: ready[t] if t in ready else repeated(t, s) for t in range(s, blocks)}
        early = range(s + 1, min(s + 1 + EARLY, blocks))
        ready = {t: repeated(t, s + 1) for t in early}
        upper = [over_rows(a[s], k) for k in range(8)]
        side = [over_rows(e[s], k) for k in range(8)]
        for k in range(8):
            pivot = lax.rsqrt(over_rows(columns[s][k], k))
            for t in range(s, blocks):
                columns[t][k] = columns[t][k] * pivot
            upper[k] = upper[k] * pivot
            side[k] = side[k] * pivot
            for m in range(k + 1, 8):
                factor = over_rows(columns[s][k], m)
                for t in range(s, blocks):
                    columns[t][m] = columns[t][m] - columns[t][k] * factor
                upper[m] = upper[m] - upper[k] * factor
                side[m] = side[m] - side[k] * factor
            if s + 1 < blocks:
                for j in range(8):
                    factor = over_rows(columns[s + 1][k], j)
                    for t in early:
                        ready[t][j] = ready[t][j] - columns[t][k] * factor
        for t in range(s + 1, blocks):
            for k in range(8):
                a[t] = a[t] - columns[t][k] * upper[k]
                e[t] = e[t] - columns[t][k] * side[k]
        for k in range(1, 8):
            upper[0] = jnp.where(rows >= k, upper[k], upper[0])
            side[0] = jnp.where(rows >= k, side[k], side[0])
        a_ref[8 * s : 8 * s + 8, :] = jnp.where(lanes >= rows + 8 * s, upper[0], 0.0)
        e_ref[8 * s : 8 * s + 8, :] = side[0]


def factor_steps(work, r_ref, x_ref, tile_a, tile_e):
    size = work.shape[0]
    blocks = size // TILE
    r_ref[...] = jnp.zeros((size, size), jnp.float32)
    x_ref[...] = jnp.zeros((size, size), jnp.float32)

    def block_step(b, carry):
        spot = pl.ds(pl.multiple_of(b * TILE, TILE), TILE)
        tile_a[...] = work[spot, spot]
        factor_tile(tile_a, tile_e)
        r_ref[spot, spot] = tile_a[...]
        x_ref[spot, spot] = tile_e[...]
        for at in range(blocks):
            here, rest = slice(TILE * at, TILE * at + TILE), slice(TILE * at + TILE, size)

            @pl.when(b == at)
            def _():
                inverse = pieces(tile_e[...])
                if at > 0:
                    done = slice(0, TILE * at)
                    x_ref[here, done] = close_dot(inverse, pieces(x_ref[here, done]), PLAIN)
                if at < blocks - 1:
                    right = close_dot(inverse, pieces(work[here, rest]), PLAIN)
                    r_ref[here, rest] = right
                    right = pieces(right)
                    work[rest, rest] = work[rest, rest] - close_dot(right, right, ACROSS)
                    done = slice(0, TILE * at + TILE)
                    x_ref[rest, done] = x_ref[rest, done] - close_dot(right, pieces(x_ref[here, done]), ACROSS)

        return carry

    lax.fori_loop(0, blocks, block_step, 0)


def factor_scratch(size):
    return [pltpu.VMEM((size, size), jnp.float32)] + [pltpu.VMEM((TILE, TILE), jnp.float32)] * 2


def factor_kernel(g_ref, r_ref, x_ref, work, tile_a, tile_e):
    work[...] = g_ref[...]
    factor_steps(work, r_ref, x_ref, tile_a, tile_e)


def factorize(gram):
    size = gram.shape[0]
    square = jax.ShapeDtypeStruct((size, size), jnp.float32)
    return pl.pallas_call(
        factor_kernel,
        in_specs=[VMEM],
        out_specs=[VMEM, VMEM],
        out_shape=[square, square],
        scratch_shapes=factor_scratch(size),
        compiler_params=PARAMS,
    )(gram)


def pair_kernel(count, g_ref, r_ref, own_ref, other_ref, work, tile_a, tile_e, r_all, x_all):
    rows = r_ref.shape[0]
    share = rows // count
    work[rows:, :rows] = jnp.zeros((rows, rows), jnp.float32)
    for place in range(count):
        start = pl.multiple_of(block_at(place, count) * share, share)
        here = slice(share * place, share * place + share)
        work[pl.ds(start, share), :] = g_ref[here, : 2 * rows]
        work[pl.ds(rows + start, share), rows:] = g_ref[here, 2 * rows :]
    factor_steps(work, r_all, x_all, tile_a, tile_e)
    is_first = lax.axis_index("probe") == 0

    @pl.when(is_first)
    def _():
        r_ref[...] = r_all[:rows, :]
        own_ref[...] = x_all[:rows, :rows]
        other_ref[...] = jnp.zeros((rows, rows), jnp.float32)

    @pl.when(jnp.logical_not(is_first))
    def _():
        r_ref[...] = r_all[rows:, :]
        own_ref[...] = x_all[rows:, rows:]
        other_ref[...] = x_all[rows:, :rows]


def factorize_pair(travelled, count):
    rows = travelled.shape[0]
    square = jax.ShapeDtypeStruct((rows, rows), jnp.float32)
    return pl.pallas_call(
        functools.partial(pair_kernel, count),
        in_specs=[VMEM],
        out_specs=[VMEM] * 3,
        out_shape=[jax.ShapeDtypeStruct((rows, 2 * rows), jnp.float32), square, square],
        scratch_shapes=factor_scratch(2 * rows) + [pltpu.VMEM((2 * rows, 2 * rows), jnp.float32)] * 2,
        compiler_params=PARAMS,
    )(travelled)


def basis_kernel(own_ref, other_ref, first_ref, second_ref, front_ref, back_ref, out_ref):
    half = first_ref.shape[2]
    own, other = pieces(own_ref[...]), pieces(other_ref[...])
    for at, (mine, theirs) in enumerate(((first_ref, front_ref), (second_ref, back_ref))):
        out_ref[0, :, half * at : half * at + half] = close_dot(own, pieces(mine[0]), PLAIN) + close_dot(
            other, pieces(theirs[0]), PLAIN
        )


def basis_of(own, other, first, second, front, back):
    _, rows, half = first.shape
    weights = pl.BlockSpec((rows, rows), lambda k: (0, 0))
    panel = pl.BlockSpec((1, rows, half), lambda k: (k, 0, 0))
    return pl.pallas_call(
        basis_kernel,
        grid=(3,),
        in_specs=[weights] * 2 + [panel] * 4,
        out_specs=pl.BlockSpec((1, rows, 2 * half), lambda k: (k, 0, 0)),
        out_shape=jax.ShapeDtypeStruct((3, rows, 2 * half), jnp.float32),
        compiler_params=PARAMS,
    )(own, other, first, second, front, back)


def partners(axis, bit):
    return [(i, i ^ bit) for i in range(lax.axis_size(axis))]


def bits_of(axis):
    bits, bit = [], 1
    while bit < lax.axis_size(axis):
        bits.append(bit)
        bit *= 2
    return bits


def scatter_sum(block, axis):
    for bit in bits_of(axis):
        half = block.shape[0] // 2
        block = block[:half] + lax.ppermute(block[half:], axis, partners(axis, bit))
    return block


def gather_back(block, axis):
    for bit in reversed(bits_of(axis)):
        block = jnp.concatenate([block, lax.ppermute(block, axis, partners(axis, bit))], 0)
    return block


def swapped(block):
    return lax.ppermute(block, "probe", [(0, 1), (1, 0)])


def pair_body(probes, coefs, offsets):
    _, columns, cells = probes.shape
    slabs = lax.axis_size("slab")
    scale = 1.0 / (3 * cells * slabs)
    is_first = lax.axis_index("probe") == 0
    half = cells // 2
    start = lax.axis_index("probe") * half
    theirs = swapped(lax.dynamic_slice_in_dim(probes, start, half, 2))
    first, mid, last = pack_edges(probes, coefs)
    forward = [(i, i + 1) for i in range(slabs - 1)]
    low = lax.ppermute(last, "slab", forward)
    high = lax.ppermute(first, "slab", [(b, a) for a, b in forward])
    ends = swapped(jnp.where(is_first, jnp.concatenate([low, mid], 0), jnp.concatenate([mid, high], 0)))
    front, back, gram = panel_of(probes, coefs, low, high, offsets, scale)
    their_back = lax.ppermute(back, "probe", [(0, 1)])
    half_coefs = jnp.where(is_first, coefs[:, half:], coefs[:, :half])
    their_front, sums = cross_of(
        theirs, half_coefs, ends[: 4 * HALO], ends[4 * HALO :], offsets, front, back, gram, scale, slabs
    )
    share = scatter_sum(sums, "slab")
    other = swapped(share)
    share = jnp.concatenate(
        [
            jnp.where(is_first, share[:, :columns], other[:, :columns]),
            share[:, columns:] + other[:, columns:],
            jnp.where(is_first, other[:, :columns], share[:, :columns]),
        ],
        1,
    )
    r_rows, own, other = factorize_pair(gather_back(share, "slab"), slabs)
    return basis_of(own, other, front, back, their_front, their_back), r_rows


def whole_body(probes, coefs, offsets):
    _, columns, cells = probes.shape
    slabs, groups = lax.axis_size("slab"), lax.axis_size("probe")
    me = lax.axis_index("probe")
    scale = 1.0 / (3 * cells * slabs)
    first, _, last = pack_edges(probes, coefs)
    forward = [(i, i + 1) for i in range(slabs - 1)]
    low = lax.ppermute(last, "slab", forward)
    high = lax.ppermute(first, "slab", [(b, a) for a, b in forward])
    front, back, _ = panel_of(probes, coefs, low, high, offsets, scale)
    panel = jnp.concatenate([front, back], 2)
    everyone = lax.all_gather(panel, "probe", axis=1, tiled=True)
    part = scale * jnp.einsum("kpc,kqc->pq", panel, everyone, precision=CLOSE)
    gram = lax.all_gather(lax.psum(part, "slab"), "probe", axis=0, tiled=True)
    upper, inverse = factorize(gram)
    mine = lax.dynamic_slice_in_dim(inverse, me * columns, columns, 0)
    basis = jnp.einsum("pq,kqc->kpc", mine, everyone, precision=CLOSE)
    return basis, lax.dynamic_slice_in_dim(upper, me * columns, columns, 0)


def body(probes, viscosity, coupling, misfit_weight, band_offsets):
    coefs = jnp.concatenate([coupling.reshape(TERMS, -1), viscosity[None, :], misfit_weight], 0)
    run = pair_body if lax.axis_size("probe") == 2 else whole_body
    return run(probes, coefs, band_offsets)


def solution(mesh):
    return jax.shard_map(
        body,
        mesh=mesh,
        in_specs=(
            P(None, "probe", "slab"),
            P("slab"),
            P(None, None, None, "slab"),
            P(None, "slab"),
            P(),
        ),
        out_specs=(P(None, "probe", "slab"), P("probe", None)),
        check_vma=False,
    )
```

```python
import functools

import jax
import jax.numpy as jnp
from jax import lax
from jax.experimental import pallas as pl
from jax.experimental.pallas import tpu as pltpu
from jax.sharding import PartitionSpec as P

REACH = 4
BANDS = 4
HALO = 4 * REACH
TERMS = 9 * BANDS
COEFS = TERMS + 4
TILE = 128
EARLY = 1
AT_ONCE = 8
EXACT = lax.Precision.HIGHEST
CLOSE = lax.Precision.HIGH
VMEM = pl.BlockSpec(memory_space=pltpu.VMEM)


def taking(micros):
    return pl.CostEstimate(flops=0, transcendentals=0, bytes_accessed=int(micros * 3.5e6))


PARAMS = pltpu.CompilerParams(vmem_limit_bytes=48 * 2**20)


def pack_kernel(x_ref, coef_ref, low_ref, mid_ref, high_ref, tiles_ref, sems):
    rows, cells = x_ref.shape[1], coef_ref.shape[1]
    blank = jnp.zeros((rows - COEFS, TILE), jnp.float32)
    is_first = lax.axis_index("probe") == 0
    middle = jnp.where(is_first, cells // 4, cells // 4 * 3 - TILE)
    starts = (0, pl.multiple_of(middle, TILE), cells - TILE)
    copies = [
        pltpu.make_async_copy(x_ref.at[:, :, pl.ds(start, TILE)], tiles_ref.at[at], sems.at[at])
        for at, start in enumerate(starts)
    ]
    for copy in copies:
        copy.start()
    for copy in copies:
        copy.wait()

    def pack(out_ref, at, spot):
        for comp in range(3):
            out_ref[HALO * comp : HALO * comp + HALO, :] = tiles_ref[at, comp].T[spot]
        coef = jnp.concatenate([coef_ref[:, pl.ds(starts[at], TILE)], blank], 0)
        out_ref[3 * HALO : 4 * HALO, :] = coef.T[spot]

    head, tail = slice(0, HALO), slice(TILE - HALO, TILE)
    pack(low_ref, 0, head)
    pack(high_ref, 2, tail)

    @pl.when(is_first)
    def _():
        pack(mid_ref, 1, head)

    @pl.when(jnp.logical_not(is_first))
    def _():
        pack(mid_ref, 1, tail)


def pack_edges(probes, coefs):
    _, rows, cells = probes.shape
    edge = jax.ShapeDtypeStruct((4 * HALO, rows), jnp.float32)
    return pl.pallas_call(
        pack_kernel,
        in_specs=[pl.BlockSpec(memory_space=pltpu.HBM), VMEM],
        out_specs=[VMEM] * 3,
        out_shape=[edge] * 3,
        scratch_shapes=[pltpu.VMEM((3, 3, rows, TILE), jnp.float32), pltpu.SemaphoreType.DMA((3,))],
        compiler_params=PARAMS,
    )(probes, coefs)


def turned(x, amount):
    if isinstance(amount, int):
        return pltpu.roll(x, (TILE - amount) % TILE, 1)
    return pltpu.roll(x, lax.rem(TILE - amount, TILE), 1)


def moved(tiles, amount, lane):
    turns = [turned(t, amount) for t in tiles]
    return [
        jnp.where(lane < TILE - amount, turns[i], turns[min(i + 1, len(tiles) - 1)])
        for i in range(len(tiles))
    ]


def stretch(tiles, lane):
    turns = [turned(t, TILE - HALO) for t in tiles]
    return [jnp.where(lane < HALO, turns[i], turns[i + 1]) for i in range(len(tiles) - 1)]


def segment_steps(x_at, coef_at, count, off_ref, x_ref, coef_ref, edges, out_refs, scratch):
    rows = edges[0].shape[1]
    tab_ref, mid_ref, in_ref, ends_ref, *fetched = scratch
    if fetched:
        here_ref, sem = fetched
        fetch = pltpu.make_async_copy(x_ref, here_ref, sem)
        fetch.start()
    lane = lax.broadcasted_iota(jnp.int32, (8, TILE), 1)
    given = [off_ref[b] for b in range(BANDS)]
    slots = [sum((other < off).astype(jnp.int32) for other in given) for off in given]
    offs = [sum(jnp.where(slot == r, off, 0) for slot, off in zip(slots, given)) for r in range(BANDS)]
    offs[0], offs[-1] = -REACH, REACH
    me = lax.axis_index("probe")
    x_first, coef_first = x_at(me), coef_at(me)

    coef_low_ref, coef_high_ref = edges
    blank = jnp.zeros((TILE - HALO, rows), jnp.float32)
    for comp in range(4):
        start = HALO * comp
        low, high = coef_low_ref[start : start + HALO, :], coef_high_ref[start : start + HALO, :]
        if comp < 3 and not fetched:
            start += 3 * rows
            low, high = x_ref[start : start + HALO, :], x_ref[start + 3 * HALO : start + 4 * HALO, :]
        ends_ref[comp] = jnp.concatenate([blank, low], 0).T
        ends_ref[4 + comp] = jnp.concatenate([high, blank], 0).T

    def tiles_of(load, first, total, comp, spot):
        def at(i):
            start = i * TILE
            return load(pl.ds(start if isinstance(i, int) else pl.multiple_of(start, TILE), TILE))

        def edge(is_end, which, i):
            halo = ends_ref[which + comp, spot, :]
            if isinstance(first, int):
                return halo if is_end else at(i)
            return jnp.where(is_end, halo, at(jnp.clip(i, 0, total - 1)))

        return (
            [edge(first == 0, 0, first - 1)]
            + [at(first + i) for i in range(count)]
            + [edge(first + count == total, 4, first + count)]
        )

    for group in range(COEFS // 8):
        spot = slice(8 * group, 8 * group + 8)
        coef_total = coef_ref.shape[1] // TILE
        ext = stretch(
            tiles_of(lambda where: coef_ref[spot, where], coef_first, coef_total, 3, spot), lane
        )
        by_step = {(0, b): moved(ext, REACH, lane) for b in range(BANDS)}
        by_step.update({(2, b): moved(ext, 3 * REACH, lane) for b in range(BANDS)})
        for b in range(BANDS):
            by_step[1, b] = moved(ext, 2 * REACH - given[b], lane)
            by_step[3, b] = moved(ext, 4 * REACH - given[b], lane)
        for j in range(8):
            row = 8 * group + j
            if row >= TERMS:
                continue
            for step in range(4):
                for i in range(count + 1):
                    tile = by_step[step, row // 9][i]
                    tab_ref[step, 9 * slots[row // 9] + row % 9, :, TILE * i : TILE * i + TILE] = jnp.broadcast_to(
                        tile[j : j + 1, :], (8, TILE)
                    )
        if group == COEFS // 8 - 1:
            for half, step in enumerate((0, 2)):
                for i in range(count + 1):
                    tile = by_step[step, 0][i]
                    visc = jnp.broadcast_to(tile[4:5, :], (8, TILE))
                    for comp in range(3):
                        weight = jnp.broadcast_to(tile[5 + comp : 6 + comp, :], (8, TILE))
                        mid_ref[half, comp, :, TILE * i : TILE * i + TILE] = visc * visc * weight
            between = moved(ext, 2 * REACH, lane)
            for at, i in enumerate((0, count)):
                inside = jnp.broadcast_to(between[i][4:5, :], (8, TILE)) != 0.0
                in_ref[at] = jnp.where(inside, 1.0, 0.0)

    def apply(tiles, step, outs):
        sign = 1 if step % 2 == 0 else -1
        result = [[[], [], []] for _ in range(AT_ONCE)]
        amounts = [REACH] + [REACH + sign * off for off in offs]
        masks = [lane < TILE - amount for amount in amounts]

        def turns_of(i):
            return [
                [
                    [row[i] if isinstance(amount, int) and amount == 0 else turned(row[i], amount) for amount in amounts]
                    for row in tiles[at]
                ]
                for at in range(AT_ONCE)
            ]

        ahead = turns_of(0)
        for i in range(outs):
            here = ahead
            ahead = turns_of(i + 1) if i + 1 < len(tiles[0][0]) else here
            spot = slice(TILE * i, TILE * i + TILE)
            shifted = [
                [
                    [
                        here[at][m][j]
                        if isinstance(amounts[j], int) and amounts[j] == 0
                        else jnp.where(masks[j], here[at][m][j], ahead[at][m][j])
                        for j in range(1 + BANDS)
                    ]
                    for m in range(3)
                ]
                for at in range(AT_ONCE)
            ]

            def sums(k):
                total = [shifted[at][k][0] for at in range(AT_ONCE)]
                for b in range(BANDS):
                    for m in range(3):
                        term = 9 * b + (3 * k + m if sign == 1 else 3 * m + k)
                        table = tab_ref[step, term, :, spot]
                        total = [total[at] + table * shifted[at][m][1 + b] for at in range(AT_ONCE)]
                return total

            for k in range(3):
                total = sums(k)
                if step % 2 == 0:
                    middle = mid_ref[step // 2, k, :, spot]
                    total = [x * middle for x in total]
                if step == 1 and i in (0, count):
                    inside = in_ref[0 if i == 0 else 1]
                    total = [x * inside for x in total]
                for at in range(AT_ONCE):
                    result[at][k].append(total[at])
        return result

    def group_step(g, carry):
        spots = [pl.ds(pl.multiple_of(8 * (AT_ONCE * g + at), 8), 8) for at in range(AT_ONCE)]
        total = x_ref.shape[-1] // TILE

        def load(m, at, where):
            if fetched:
                return here_ref[m, spots[at], where]
            return x_ref[pl.ds(pl.multiple_of(m * rows + 8 * (AT_ONCE * g + at), 8), 8), where]

        tiles = [
            [
                stretch(
                    tiles_of(functools.partial(load, m, at), x_first, total, m, spot), lane
                )
                for m in range(3)
            ]
            for at, spot in enumerate(spots)
        ]
        for step in range(4):
            tiles = apply(tiles, step, count + 1 if step < 3 else count)
        for at, spot in enumerate(spots):
            for m in range(3):
                for i in range(count // len(out_refs)):
                    here = slice(TILE * i, TILE * i + TILE)
                    if len(out_refs) == 1:
                        out_refs[0][m, spot, here] = tiles[at][m][i]
                    else:
                        one, two = tiles[at][m][i], tiles[at][m][count // 2 + i]
                        out_refs[0][m, spot, here] = jnp.where(me == 0, one, two)
                        out_refs[1][m, spot, here] = jnp.where(me == 0, two, one)
        return carry

    if fetched:
        fetch.wait()
    lax.fori_loop(0, rows // (8 * AT_ONCE), group_step, 0)


def segment_scratch(rows, count):
    wide = (count + 1) * TILE
    return [
        pltpu.VMEM((4, TERMS, 8, wide), jnp.float32),
        pltpu.VMEM((2, 3, 8, wide), jnp.float32),
        pltpu.VMEM((2, 8, TILE), jnp.float32),
        pltpu.VMEM((8, rows, TILE), jnp.float32),
    ]


SMEM = pl.BlockSpec(memory_space=pltpu.SMEM)


def pieces(x):
    high = x.astype(jnp.bfloat16)
    return high, (x - high.astype(jnp.float32)).astype(jnp.bfloat16)


def close_dot(left, right, over):
    dot = functools.partial(lax.dot_general, dimension_numbers=((over, ((), ()))), preferred_element_type=jnp.float32)
    return dot(left[0], right[0]) + (dot(left[0], right[1]) + dot(left[1], right[0]))


ALONG = ((1,), (1,))
PLAIN = ((1,), (0,))
ACROSS = ((0,), (0,))


def products(left, right):
    total = None
    for k in range(3):
        part = close_dot(pieces(left[k]), pieces(right[k]), ALONG)
        total = part if total is None else total + part
    return total


def own_products(refs):
    dot = functools.partial(lax.dot_general, dimension_numbers=(ALONG, ((), ())), preferred_element_type=jnp.float32)
    main = mixed = None
    for ref in refs:
        for k in range(3):
            high, low = pieces(ref[k])
            one, two = dot(high, high), dot(high, low)
            main, mixed = (one, two) if main is None else (main + one, mixed + two)
    return main + (mixed + mixed.T)


def segment_kernel(x_at, coef_at, count, parts, scale, off_ref, x_ref, coef_ref, *refs):
    edges, refs = refs[:2], refs[2:]
    rest, refs = (refs[:2], refs[2:]) if scale else ((), refs)
    out_refs, refs = refs[:parts], refs[parts:]
    gram_ref, refs = (refs[0], refs[1:]) if scale else (None, refs)
    segment_steps(x_at, coef_at, count, off_ref, x_ref, coef_ref, edges, out_refs, refs)
    if scale:
        gram_ref[...] = own_products((*out_refs, *rest)) * scale


def segment(x_at, coef_at, count, offsets, x, coefs, edges, parts=1, rest=(), scale=None):
    rows = edges[0].shape[1]
    scratch, place = segment_scratch(rows, count), VMEM
    if x.ndim == 3:
        place = pl.BlockSpec(memory_space=pltpu.HBM)
        scratch += [pltpu.VMEM(x.shape, jnp.float32), pltpu.SemaphoreType.DMA(())]
    shapes = [jax.ShapeDtypeStruct((3, rows, count * TILE // parts), jnp.float32)] * parts
    if scale:
        shapes.append(jax.ShapeDtypeStruct((rows, rows), jnp.float32))
    result = pl.pallas_call(
        functools.partial(segment_kernel, x_at, coef_at, count, parts, scale),
        in_specs=[SMEM, place] + [VMEM] * (1 + len(edges) + len(rest)),
        out_specs=[VMEM] * len(shapes),
        out_shape=shapes,
        scratch_shapes=scratch,
        compiler_params=PARAMS,
        cost_estimate=taking(2 + 2 * (count + 1) * rows / 256),
    )(offsets, x, coefs, *edges, *rest)
    return result if len(shapes) > 1 else result[0]


def reversed_bits(place, count):
    result, bit = 0, 1
    while bit < count:
        result = 2 * result + (place // bit) % 2
        bit *= 2
    return result


def block_at(place, count):
    return lax.bitwise_xor(lax.rem(lax.axis_index("slab"), count), jnp.int32(reversed_bits(place, count)))


def cross_kernel(scale, count, own_ref, raw_ref, ready_ref, gram_ref, out_ref, work):
    rows = gram_ref.shape[0]
    quarter = raw_ref.shape[2]
    is_first = lax.axis_index("probe") == 0

    @pl.when(is_first)
    def _():
        near, far = own_ref.at[:, :, :quarter], own_ref.at[:, :, quarter:]
        work[...] = (products(near, ready_ref) + products(far, raw_ref)) * scale

    @pl.when(jnp.logical_not(is_first))
    def _():
        near, far = own_ref.at[:, :, :quarter], own_ref.at[:, :, quarter:]
        work[...] = (products(raw_ref, near) + products(ready_ref, far)) * scale

    share = rows // count
    for place in range(count):
        spot = pl.ds(pl.multiple_of(block_at(place, count) * share, share), share)
        out_ref[share * place : share * place + share, :rows] = gram_ref[spot, :]
        out_ref[share * place : share * place + share, rows:] = work[spot, :]


def cross_of(own, raw, ready, gram, scale, count):
    _, rows, _ = own.shape
    return pl.pallas_call(
        functools.partial(cross_kernel, scale, count),
        in_specs=[VMEM] * 4,
        out_specs=VMEM,
        out_shape=jax.ShapeDtypeStruct((rows, 2 * rows), jnp.float32),
        scratch_shapes=[pltpu.VMEM((rows, rows), jnp.float32)],
        compiler_params=PARAMS,
    )(own, raw, ready, gram)


def over_lanes(x, j):
    return jnp.broadcast_to(x[:, j : j + 1], (8, TILE))


def over_rows(x, i):
    return jnp.broadcast_to(x[i : i + 1, :], (8, TILE))


def factor_tile(a_ref, e_ref):
    blocks = TILE // 8
    rows = lax.broadcasted_iota(jnp.int32, (8, TILE), 0)
    lanes = lax.broadcasted_iota(jnp.int32, (8, TILE), 1)
    a = [a_ref[8 * t : 8 * t + 8, :] for t in range(blocks)]
    e = [jnp.where(lanes == rows + 8 * t, 1.0, 0.0) for t in range(blocks)]

    def repeated(t, s):
        return [over_lanes(a[t], 8 * s + j) for j in range(8)]

    ready = {}
    for s in range(blocks):
        columns = {t: ready[t] if t in ready else repeated(t, s) for t in range(s, blocks)}
        early = range(s + 1, min(s + 1 + EARLY, blocks))
        ready = {t: repeated(t, s + 1) for t in early}
        upper = [over_rows(a[s], k) for k in range(8)]
        side = [over_rows(e[s], k) for k in range(8)]
        for k in range(8):
            pivot = lax.rsqrt(over_rows(columns[s][k], k))
            for t in range(s, blocks):
                columns[t][k] = columns[t][k] * pivot
            upper[k] = upper[k] * pivot
            side[k] = side[k] * pivot
            for m in range(k + 1, 8):
                factor = over_rows(columns[s][k], m)
                for t in range(s, blocks):
                    columns[t][m] = columns[t][m] - columns[t][k] * factor
                upper[m] = upper[m] - upper[k] * factor
                side[m] = side[m] - side[k] * factor
            if s + 1 < blocks:
                for j in range(8):
                    factor = over_rows(columns[s + 1][k], j)
                    for t in early:
                        ready[t][j] = ready[t][j] - columns[t][k] * factor
        for t in range(s + 1, blocks):
            for k in range(8):
                a[t] = a[t] - columns[t][k] * upper[k]
                e[t] = e[t] - columns[t][k] * side[k]
        for k in range(1, 8):
            upper[0] = jnp.where(rows >= k, upper[k], upper[0])
            side[0] = jnp.where(rows >= k, side[k], side[0])
        a_ref[8 * s : 8 * s + 8, :] = jnp.where(lanes >= rows + 8 * s, upper[0], 0.0)
        e_ref[8 * s : 8 * s + 8, :] = side[0]


def factor_steps(work, r_ref, x_ref, tile_a, tile_e):
    size = work.shape[0]
    blocks = size // TILE
    r_ref[...] = jnp.zeros((size, size), jnp.float32)
    x_ref[...] = jnp.zeros((size, size), jnp.float32)

    def block_step(b, carry):
        spot = pl.ds(pl.multiple_of(b * TILE, TILE), TILE)
        tile_a[...] = work[spot, spot]
        factor_tile(tile_a, tile_e)
        r_ref[spot, spot] = tile_a[...]
        x_ref[spot, spot] = tile_e[...]
        for at in range(blocks):
            here, rest = slice(TILE * at, TILE * at + TILE), slice(TILE * at + TILE, size)

            @pl.when(b == at)
            def _():
                inverse = pieces(tile_e[...])
                if at > 0:
                    done = slice(0, TILE * at)
                    x_ref[here, done] = close_dot(inverse, pieces(x_ref[here, done]), PLAIN)
                if at < blocks - 1:
                    right = close_dot(inverse, pieces(work[here, rest]), PLAIN)
                    r_ref[here, rest] = right
                    right = pieces(right)
                    work[rest, rest] = work[rest, rest] - close_dot(right, right, ACROSS)
                    done = slice(0, TILE * at + TILE)
                    x_ref[rest, done] = x_ref[rest, done] - close_dot(right, pieces(x_ref[here, done]), ACROSS)

        return carry

    lax.fori_loop(0, blocks, block_step, 0)


def factor_scratch(size):
    return [pltpu.VMEM((size, size), jnp.float32)] + [pltpu.VMEM((TILE, TILE), jnp.float32)] * 2


def factor_kernel(g_ref, r_ref, x_ref, work, tile_a, tile_e):
    work[...] = g_ref[...]
    factor_steps(work, r_ref, x_ref, tile_a, tile_e)


def factorize(gram):
    size = gram.shape[0]
    square = jax.ShapeDtypeStruct((size, size), jnp.float32)
    return pl.pallas_call(
        factor_kernel,
        in_specs=[VMEM],
        out_specs=[VMEM, VMEM],
        out_shape=[square, square],
        scratch_shapes=factor_scratch(size),
        compiler_params=PARAMS,
    )(gram)


def pair_kernel(count, g_ref, r_ref, own_ref, other_ref, work, tile_a, tile_e, r_all, x_all):
    rows = r_ref.shape[0]
    share = rows // count
    work[rows:, :rows] = jnp.zeros((rows, rows), jnp.float32)
    for place in range(count):
        start = pl.multiple_of(block_at(place, count) * share, share)
        here = slice(share * place, share * place + share)
        work[pl.ds(start, share), :] = g_ref[here, : 2 * rows]
        work[pl.ds(rows + start, share), rows:] = g_ref[here, 2 * rows :]
    factor_steps(work, r_all, x_all, tile_a, tile_e)
    is_first = lax.axis_index("probe") == 0

    @pl.when(is_first)
    def _():
        r_ref[...] = r_all[:rows, :]
        own_ref[...] = x_all[:rows, :rows]
        other_ref[...] = jnp.zeros((rows, rows), jnp.float32)

    @pl.when(jnp.logical_not(is_first))
    def _():
        r_ref[...] = r_all[rows:, :]
        own_ref[...] = x_all[rows:, rows:]
        other_ref[...] = x_all[rows:, :rows]


def factorize_pair(travelled, count):
    rows = travelled.shape[0]
    square = jax.ShapeDtypeStruct((rows, rows), jnp.float32)
    return pl.pallas_call(
        functools.partial(pair_kernel, count),
        in_specs=[VMEM],
        out_specs=[VMEM] * 3,
        out_shape=[jax.ShapeDtypeStruct((rows, 2 * rows), jnp.float32), square, square],
        scratch_shapes=factor_scratch(2 * rows) + [pltpu.VMEM((2 * rows, 2 * rows), jnp.float32)] * 2,
        compiler_params=PARAMS,
        cost_estimate=taking(15),
    )(travelled)


def basis_kernel(own_ref, other_ref, outer_ref, inner_ref, half_ref, raw_ref, ready_ref, early_ref, late_ref, out_ref):
    me = lax.axis_index("probe")
    quarter = outer_ref.shape[2]
    own = pieces(own_ref[...])
    starts = (me * 3 * quarter, (1 + me) * quarter, (1 - me) * 2 * quarter)
    for start, ref in zip(starts, (outer_ref, inner_ref, half_ref)):
        spot = pl.ds(pl.multiple_of(start, TILE), ref.shape[2])
        out_ref[0, :, spot] = close_dot(own, pieces(ref[0]), PLAIN)

    @pl.when(me == 1)
    def _():
        other = pieces(other_ref[...])
        for at, ref in enumerate((raw_ref, ready_ref, early_ref, late_ref)):
            spot = slice(quarter * at, quarter * at + quarter)
            out_ref[0, :, spot] = out_ref[0, :, spot] + close_dot(other, pieces(ref[0]), PLAIN)


def basis_of(own, other, outer, inner, half, raw, ready, early, late):
    _, rows, quarter = outer.shape
    weights = pl.BlockSpec((rows, rows), lambda k: (0, 0))
    short = pl.BlockSpec((1, rows, quarter), lambda k: (k, 0, 0))
    wide = pl.BlockSpec((1, rows, 2 * quarter), lambda k: (k, 0, 0))
    return pl.pallas_call(
        basis_kernel,
        grid=(3,),
        in_specs=[weights, weights, short, short, wide, short, short, short, short],
        out_specs=pl.BlockSpec((1, rows, 4 * quarter), lambda k: (k, 0, 0)),
        out_shape=jax.ShapeDtypeStruct((3, rows, 4 * quarter), jnp.float32),
        compiler_params=PARAMS,
    )(own, other, outer, inner, half, raw, ready, early, late)


def partners(axis, bit):
    return [(i, i ^ bit) for i in range(lax.axis_size(axis))]


def bits_of(axis):
    bits, bit = [], 1
    while bit < lax.axis_size(axis):
        bits.append(bit)
        bit *= 2
    return bits


def split_bits(axis):
    bits = bits_of(axis)
    return bits[: max(len(bits) - 2, 0)], bits[max(len(bits) - 2, 0) :]


def scatter_sum(block, axis):
    halved, whole = split_bits(axis)
    for bit in halved:
        half = block.shape[0] // 2
        block = block[:half] + lax.ppermute(block[half:], axis, partners(axis, bit))
    for bit in whole:
        block = block + lax.ppermute(block, axis, partners(axis, bit))
    return block


def gather_back(block, axis):
    for bit in reversed(split_bits(axis)[0]):
        block = jnp.concatenate([block, lax.ppermute(block, axis, partners(axis, bit))], 0)
    return block


def swapped(block):
    return lax.ppermute(block, "probe", [(0, 1), (1, 0)])


def halo_of(first, last):
    slabs = lax.axis_size("slab")
    forward = [(i, i + 1) for i in range(slabs - 1)]
    return lax.ppermute(last, "slab", forward), lax.ppermute(first, "slab", [(b, a) for a, b in forward])


def pair_body(probes, coefs, offsets):
    _, columns, cells = probes.shape
    slabs = lax.axis_size("slab")
    scale = 1.0 / (3 * cells * slabs)
    me = lax.axis_index("probe")
    is_first = me == 0
    quarter = cells // 4
    tiles = quarter // TILE

    first, mid, last = pack_edges(probes, coefs)
    low, high = halo_of(first, last)
    pack = 3 * HALO
    ends = jnp.where(
        is_first,
        jnp.concatenate([low[:pack], mid[:pack]], 0),
        jnp.concatenate([mid[:pack], high[:pack]], 0),
    )
    sent = lax.dynamic_slice_in_dim(probes, me * 3 * quarter, quarter, 2).reshape(3 * columns, quarter)
    theirs = swapped(jnp.concatenate([sent, ends], 0))
    run = functools.partial(segment, offsets=offsets, coefs=coefs)

    def at_half(me):
        return me * 2 * tiles

    def at_other_half(me):
        return (1 - me) * 2 * tiles

    def at_raw(me):
        return (1 - me) * 3 * tiles

    edges = (low, high)
    outer, inner = run(at_half, at_half, 2 * tiles, x=probes, edges=edges, parts=2)
    ready = swapped(inner)
    half, gram = run(
        at_other_half, at_other_half, 2 * tiles, x=probes, edges=edges, rest=(inner, outer), scale=scale
    )
    rest = (half[:, :, :quarter], half[:, :, quarter:])
    early = lax.ppermute(rest[0], "probe", [(0, 1)])
    raw = run(lambda me: 0, at_raw, tiles, x=theirs, edges=edges)
    count = 1 << len(split_bits("slab")[0])
    sums = cross_of(half, raw, ready, gram, scale, count)
    share = scatter_sum(sums, "slab")
    share, early = lax.optimization_barrier((share, early))
    other = swapped(share)
    other, late = lax.optimization_barrier((other, rest[1]))
    late = lax.ppermute(late, "probe", [(0, 1)])
    share = jnp.concatenate(
        [
            jnp.where(is_first, share[:, :columns], other[:, :columns]),
            share[:, columns:] + other[:, columns:],
            jnp.where(is_first, other[:, :columns], share[:, :columns]),
        ],
        1,
    )
    r_rows, own, other = factorize_pair(gather_back(share, "slab"), count)
    return basis_of(own, other, outer, inner, half, raw, ready, early, late), r_rows


def whole_body(probes, coefs, offsets):
    _, columns, cells = probes.shape
    slabs = lax.axis_size("slab")
    me = lax.axis_index("probe")
    scale = 1.0 / (3 * cells * slabs)
    first, _, last = pack_edges(probes, coefs)
    low, high = halo_of(first, last)
    panel = segment(lambda me: 0, lambda me: 0, cells // TILE, offsets, probes, coefs, (low, high))
    everyone = lax.all_gather(panel, "probe", axis=1, tiled=True)
    part = scale * jnp.einsum("kpc,kqc->pq", panel, everyone, precision=CLOSE)
    gram = lax.all_gather(lax.psum(part, "slab"), "probe", axis=0, tiled=True)
    upper, inverse = factorize(gram)
    mine = lax.dynamic_slice_in_dim(inverse, me * columns, columns, 0)
    basis = jnp.einsum("pq,kqc->kpc", mine, everyone, precision=CLOSE)
    return basis, lax.dynamic_slice_in_dim(upper, me * columns, columns, 0)


def body(probes, viscosity, coupling, misfit_weight, band_offsets):
    coefs = jnp.concatenate([coupling.reshape(TERMS, -1), viscosity[None, :], misfit_weight], 0)
    run = pair_body if lax.axis_size("probe") == 2 else whole_body
    return run(probes, coefs, band_offsets)


def solution(mesh):
    return jax.shard_map(
        body,
        mesh=mesh,
        in_specs=(
            P(None, "probe", "slab"),
            P("slab"),
            P(None, None, None, "slab"),
            P(None, "slab"),
            P(),
        ),
        out_specs=(P(None, "probe", "slab"), P("probe", None)),
        check_vma=False,
    )
```

```python
import functools

import jax
import jax.numpy as jnp
from jax import lax
from jax.experimental import pallas as pl
from jax.experimental.pallas import tpu as pltpu
from jax.sharding import PartitionSpec as P

REACH = 4
BANDS = 4
HALO = 4 * REACH
TERMS = 9 * BANDS
COEFS = TERMS + 4
TILE = 128
EARLY = 1
AT_ONCE = 8
EXACT = lax.Precision.HIGHEST
CLOSE = lax.Precision.HIGH
VMEM = pl.BlockSpec(memory_space=pltpu.VMEM)


def taking(micros):
    return pl.CostEstimate(flops=0, transcendentals=0, bytes_accessed=int(micros * 3.5e6))


PARAMS = pltpu.CompilerParams(vmem_limit_bytes=48 * 2**20)


def pack_kernel(x_ref, *refs):
    given, (low_ref, mid_ref, high_ref, coef_ref, tiles_ref), held, sems = refs[:3], refs[3:8], refs[8:11], refs[11]
    rows, cells = x_ref.shape[1], coef_ref.shape[1]
    blank = jnp.zeros((rows - COEFS, TILE), jnp.float32)
    is_first = lax.axis_index("probe") == 0
    middle = jnp.where(is_first, cells // 4, cells // 4 * 3 - TILE)
    starts = (0, pl.multiple_of(middle, TILE), cells - TILE)
    copies = [
        pltpu.make_async_copy(x_ref.at[:, :, pl.ds(start, TILE)], tiles_ref.at[at], sems.at[at])
        for at, start in enumerate(starts)
    ]
    copies += [pltpu.make_async_copy(one, two, sems.at[3 + at]) for at, (one, two) in enumerate(zip(given, held))]
    for copy in copies:
        copy.start()
    for copy in copies:
        copy.wait()
    coup_ref, visc_ref, weight_ref = held
    for k in range(3):
        for m in range(3):
            start = BANDS * (3 * k + m)
            coef_ref[start : start + BANDS, :] = coup_ref[k, m]
    coef_ref[TERMS : TERMS + 1, :] = visc_ref[...]
    coef_ref[TERMS + 1 :, :] = weight_ref[...]

    def pack(out_ref, at, spot):
        for comp in range(3):
            out_ref[HALO * comp : HALO * comp + HALO, :] = tiles_ref[at, comp].T[spot]
        coef = jnp.concatenate([coef_ref[:, pl.ds(starts[at], TILE)], blank], 0)
        out_ref[3 * HALO : 4 * HALO, :] = coef.T[spot]

    head, tail = slice(0, HALO), slice(TILE - HALO, TILE)
    pack(low_ref, 0, head)
    pack(high_ref, 2, tail)

    @pl.when(is_first)
    def _():
        pack(mid_ref, 1, head)

    @pl.when(jnp.logical_not(is_first))
    def _():
        pack(mid_ref, 1, tail)


def pack_edges(probes, coupling, viscosity, misfit_weight):
    _, rows, cells = probes.shape
    edge = jax.ShapeDtypeStruct((4 * HALO, rows), jnp.float32)
    return pl.pallas_call(
        pack_kernel,
        in_specs=[pl.BlockSpec(memory_space=pltpu.HBM)] * 4,
        out_specs=[VMEM] * 4,
        out_shape=[edge] * 3 + [jax.ShapeDtypeStruct((COEFS, cells), jnp.float32)],
        scratch_shapes=[
            pltpu.VMEM((3, 3, rows, TILE), jnp.float32),
            pltpu.VMEM((3, 3, BANDS, cells), jnp.float32),
            pltpu.VMEM((1, cells), jnp.float32),
            pltpu.VMEM((3, cells), jnp.float32),
            pltpu.SemaphoreType.DMA((6,)),
        ],
        compiler_params=pltpu.CompilerParams(vmem_limit_bytes=60 * 2**20),
    )(probes, coupling.transpose(1, 2, 0, 3), viscosity[None, :], misfit_weight)


def turned(x, amount):
    if isinstance(amount, int):
        return pltpu.roll(x, (TILE - amount) % TILE, 1)
    return pltpu.roll(x, lax.rem(TILE - amount, TILE), 1)


def moved(tiles, amount, lane):
    turns = [turned(t, amount) for t in tiles]
    return [
        jnp.where(lane < TILE - amount, turns[i], turns[min(i + 1, len(tiles) - 1)])
        for i in range(len(tiles))
    ]


def stretch(tiles, lane):
    turns = [turned(t, TILE - HALO) for t in tiles]
    return [jnp.where(lane < HALO, turns[i], turns[i + 1]) for i in range(len(tiles) - 1)]


def segment_steps(x_at, coef_at, count, inward, off_ref, x_ref, coef_ref, edges, out_refs, scratch):
    rows = edges[0].shape[1]
    tab_ref, mid_ref, in_ref, ends_ref, here_ref, sem = scratch
    fetch = pltpu.make_async_copy(x_ref, here_ref, sem)
    fetch.start()
    lane = lax.broadcasted_iota(jnp.int32, (8, TILE), 1)
    given = [off_ref[b] for b in range(BANDS)]
    slots = [sum((other < off).astype(jnp.int32) for other in given) for off in given]
    offs = [sum(jnp.where(slot == r, off, 0) for slot, off in zip(slots, given)) for r in range(BANDS)]
    offs[0], offs[-1] = -REACH, REACH
    me = lax.axis_index("probe")
    x_first, coef_first = x_at(me), coef_at(me)

    coef_low_ref, coef_high_ref, *x_ends = edges
    blank = jnp.zeros((TILE - HALO, rows), jnp.float32)
    for comp in range(4):
        start = HALO * comp
        low, high = coef_low_ref[start : start + HALO, :], coef_high_ref[start : start + HALO, :]
        if comp < 3 and x_ends:
            low = x_ends[0][start : start + HALO, :]
            high = x_ends[0][start + 3 * HALO : start + 4 * HALO, :]
        ends_ref[comp] = jnp.concatenate([blank, low], 0).T
        ends_ref[4 + comp] = jnp.concatenate([high, blank], 0).T

    def tiles_of(load, first, total, comp, spot):
        def at(i):
            start = i * TILE
            return load(pl.ds(start if isinstance(i, int) else pl.multiple_of(start, TILE), TILE))

        def edge(is_end, which, i):
            halo = ends_ref[which + comp, spot, :]
            if isinstance(first, int):
                return halo if is_end else at(i)
            return jnp.where(is_end, halo, at(jnp.clip(i, 0, total - 1)))

        return (
            [edge(first == 0, 0, first - 1)]
            + [at(first + i) for i in range(count)]
            + [edge(first + count == total, 4, first + count)]
        )

    for group in range(COEFS // 8):
        spot = slice(8 * group, 8 * group + 8)
        coef_total = coef_ref.shape[1] // TILE
        ext = stretch(
            tiles_of(lambda where: coef_ref[spot, where], coef_first, coef_total, 3, spot), lane
        )
        by_step = {(0, b): moved(ext, REACH, lane) for b in range(BANDS)}
        by_step.update({(2, b): moved(ext, 3 * REACH, lane) for b in range(BANDS)})
        for b in range(BANDS):
            by_step[1, b] = moved(ext, 2 * REACH - given[b], lane)
            by_step[3, b] = moved(ext, 4 * REACH - given[b], lane)
        for j in range(8):
            row = 8 * group + j
            if row >= TERMS:
                continue
            for step in range(4):
                for i in range(count + 1):
                    tile = by_step[step, row % BANDS][i]
                    tab_ref[step, 9 * slots[row % BANDS] + row // BANDS, :, TILE * i : TILE * i + TILE] = jnp.broadcast_to(
                        tile[j : j + 1, :], (8, TILE)
                    )
        if group == COEFS // 8 - 1:
            for half, step in enumerate((0, 2)):
                for i in range(count + 1):
                    tile = by_step[step, 0][i]
                    visc = jnp.broadcast_to(tile[4:5, :], (8, TILE))
                    for comp in range(3):
                        weight = jnp.broadcast_to(tile[5 + comp : 6 + comp, :], (8, TILE))
                        mid_ref[half, comp, :, TILE * i : TILE * i + TILE] = visc * visc * weight
            between = moved(ext, 2 * REACH, lane)
            for at, i in enumerate((0, count)):
                inside = jnp.broadcast_to(between[i][4:5, :], (8, TILE)) != 0.0
                in_ref[at] = jnp.where(inside, 1.0, 0.0)

    def apply(tiles, step, outs):
        sign = 1 if step % 2 == 0 else -1
        result = [[[], [], []] for _ in range(AT_ONCE)]
        amounts = [REACH] + [REACH + sign * off for off in offs]
        masks = [lane < TILE - amount for amount in amounts]

        def turns_of(i):
            return [
                [
                    [row[i] if isinstance(amount, int) and amount == 0 else turned(row[i], amount) for amount in amounts]
                    for row in tiles[at]
                ]
                for at in range(AT_ONCE)
            ]

        ahead = turns_of(0)
        for i in range(outs):
            here = ahead
            ahead = turns_of(i + 1) if i + 1 < len(tiles[0][0]) else here
            spot = slice(TILE * i, TILE * i + TILE)
            shifted = [
                [
                    [
                        here[at][m][j]
                        if isinstance(amounts[j], int) and amounts[j] == 0
                        else jnp.where(masks[j], here[at][m][j], ahead[at][m][j])
                        for j in range(1 + BANDS)
                    ]
                    for m in range(3)
                ]
                for at in range(AT_ONCE)
            ]

            def sums(k):
                total = [shifted[at][k][0] for at in range(AT_ONCE)]
                for b in range(BANDS):
                    for m in range(3):
                        term = 9 * b + (3 * k + m if sign == 1 else 3 * m + k)
                        table = tab_ref[step, term, :, spot]
                        total = [total[at] + table * shifted[at][m][1 + b] for at in range(AT_ONCE)]
                return total

            for k in range(3):
                total = sums(k)
                if step % 2 == 0:
                    middle = mid_ref[step // 2, k, :, spot]
                    total = [x * middle for x in total]
                if step == 1 and i in (0, count):
                    inside = in_ref[0 if i == 0 else 1]
                    total = [x * inside for x in total]
                for at in range(AT_ONCE):
                    result[at][k].append(total[at])
        return result

    def group_step(g, carry):
        spots = [pl.ds(pl.multiple_of(8 * (AT_ONCE * g + at), 8), 8) for at in range(AT_ONCE)]
        total = x_ref.shape[-1] // TILE

        def load(m, at, where):
            return here_ref[m, spots[at], where]

        tiles = [
            [
                stretch(
                    tiles_of(functools.partial(load, m, at), x_first, total, m, spot), lane
                )
                for m in range(3)
            ]
            for at, spot in enumerate(spots)
        ]
        for step in range(4):
            tiles = apply(tiles, step, count + 1 if step < 3 else count)
        for at, spot in enumerate(spots):
            for m in range(3):
                for i in range(count // len(out_refs)):
                    here = slice(TILE * i, TILE * i + TILE)
                    if len(out_refs) == 1:
                        out_refs[0][m, spot, here] = tiles[at][m][i]
                    else:
                        one, two = tiles[at][m][i], tiles[at][m][count // 2 + i]
                        if inward:
                            one, two = jnp.where(me == 0, one, two), jnp.where(me == 0, two, one)
                        out_refs[0][m, spot, here] = one
                        out_refs[1][m, spot, here] = two
        return carry

    fetch.wait()
    lax.fori_loop(0, rows // (8 * AT_ONCE), group_step, 0)


def segment_scratch(rows, count):
    wide = (count + 1) * TILE
    return [
        pltpu.VMEM((4, TERMS, 8, wide), jnp.float32),
        pltpu.VMEM((2, 3, 8, wide), jnp.float32),
        pltpu.VMEM((2, 8, TILE), jnp.float32),
        pltpu.VMEM((8, rows, TILE), jnp.float32),
    ]


SMEM = pl.BlockSpec(memory_space=pltpu.SMEM)


def pieces(x):
    high = x.astype(jnp.bfloat16)
    return high, (x - high.astype(jnp.float32)).astype(jnp.bfloat16)


def close_dot(left, right, over):
    dot = functools.partial(lax.dot_general, dimension_numbers=((over, ((), ()))), preferred_element_type=jnp.float32)
    return dot(left[0], right[0]) + (dot(left[0], right[1]) + dot(left[1], right[0]))


ALONG = ((1,), (1,))
PLAIN = ((1,), (0,))
ACROSS = ((0,), (0,))


def products(left, right):
    total = None
    for k in range(3):
        part = close_dot(pieces(left[k]), pieces(right[k]), ALONG)
        total = part if total is None else total + part
    return total


def own_products(refs):
    dot = functools.partial(lax.dot_general, dimension_numbers=(ALONG, ((), ())), preferred_element_type=jnp.float32)
    main = mixed = None
    for ref in refs:
        for k in range(3):
            high, low = pieces(ref[k])
            one, two = dot(high, high), dot(high, low)
            main, mixed = (one, two) if main is None else (main + one, mixed + two)
    return main + (mixed + mixed.T)


def segment_kernel(x_at, coef_at, count, parts, inward, scale, bounds, off_ref, x_ref, coef_ref, *refs):
    edges, refs = refs[:bounds], refs[bounds:]
    rest, refs = (refs[:2], refs[2:]) if scale else ((), refs)
    out_refs, refs = refs[:parts], refs[parts:]
    gram_ref, refs = (refs[0], refs[1:]) if scale else (None, refs)
    segment_steps(x_at, coef_at, count, inward, off_ref, x_ref, coef_ref, edges, out_refs, refs)
    if scale:
        gram_ref[...] = own_products((*out_refs, *rest)) * scale


def segment(x_at, coef_at, count, offsets, x, coefs, edges, ends=None, parts=1, inward=False, rest=(), scale=None):
    rows = edges[0].shape[1]
    scratch = segment_scratch(rows, count) + [pltpu.VMEM(x.shape, jnp.float32), pltpu.SemaphoreType.DMA(())]
    if ends is not None:
        edges = (*edges, ends)
    shapes = [jax.ShapeDtypeStruct((3, rows, count * TILE // parts), jnp.float32)] * parts
    if scale:
        shapes.append(jax.ShapeDtypeStruct((rows, rows), jnp.float32))
    result = pl.pallas_call(
        functools.partial(segment_kernel, x_at, coef_at, count, parts, inward, scale, len(edges)),
        in_specs=[SMEM, pl.BlockSpec(memory_space=pltpu.HBM)] + [VMEM] * (1 + len(edges) + len(rest)),
        out_specs=[VMEM] * len(shapes),
        out_shape=shapes,
        scratch_shapes=scratch,
        compiler_params=PARAMS,
        cost_estimate=taking(2 + 2 * (count + 1) * rows / 256),
    )(offsets, x, coefs, *edges, *rest)
    return result if len(shapes) > 1 else result[0]


def reversed_bits(place, count):
    result, bit = 0, 1
    while bit < count:
        result = 2 * result + (place // bit) % 2
        bit *= 2
    return result


def block_at(place, count):
    return lax.bitwise_xor(lax.rem(lax.axis_index("slab"), count), jnp.int32(reversed_bits(place, count)))


def cross_kernel(scale, count, front_ref, back_ref, raw_ref, ready_ref, gram_ref, own_ref, out_ref, work):
    rows = gram_ref.shape[0]
    is_first = lax.axis_index("probe") == 0

    @pl.when(is_first)
    def _():
        work[...] = (products(front_ref, ready_ref) + products(back_ref, raw_ref)) * scale

    @pl.when(jnp.logical_not(is_first))
    def _():
        work[...] = (products(raw_ref, front_ref) + products(ready_ref, back_ref)) * scale

    share = rows // count
    for place in range(count):
        spot = pl.ds(pl.multiple_of(block_at(place, count) * share, share), share)
        own_ref[share * place : share * place + share, :] = gram_ref[spot, :]
        out_ref[share * place : share * place + share, :] = work[spot, :]


def cross_of(front, back, raw, ready, gram, scale, count):
    rows = gram.shape[0]
    return pl.pallas_call(
        functools.partial(cross_kernel, scale, count),
        in_specs=[VMEM] * 5,
        out_specs=[VMEM] * 2,
        out_shape=[jax.ShapeDtypeStruct((rows, rows), jnp.float32)] * 2,
        scratch_shapes=[pltpu.VMEM((rows, rows), jnp.float32)],
        compiler_params=PARAMS,
    )(front, back, raw, ready, gram)


def over_lanes(x, j):
    return jnp.broadcast_to(x[:, j : j + 1], (8, TILE))


def over_rows(x, i):
    return jnp.broadcast_to(x[i : i + 1, :], (8, TILE))


def factor_tile(a_ref, e_ref):
    blocks = TILE // 8
    rows = lax.broadcasted_iota(jnp.int32, (8, TILE), 0)
    lanes = lax.broadcasted_iota(jnp.int32, (8, TILE), 1)
    a = [a_ref[8 * t : 8 * t + 8, :] for t in range(blocks)]

    def repeated(t, s):
        return [over_lanes(a[t], 8 * s + j) for j in range(8)]

    ready = {}
    for s in range(blocks):
        columns = {t: ready[t] if t in ready else repeated(t, s) for t in range(s, blocks)}
        early = range(s + 1, min(s + 1 + EARLY, blocks))
        ready = {t: repeated(t, s + 1) for t in early}
        upper = [over_rows(a[s], k) for k in range(8)]
        side = [jnp.where(lanes < 8 * s, upper[k], jnp.where(lanes == 8 * s + k, 1.0, 0.0)) for k in range(8)]
        for k in range(8):
            pivot = lax.rsqrt(over_rows(columns[s][k], k))
            for t in range(s, blocks):
                columns[t][k] = columns[t][k] * pivot
            upper[k] = upper[k] * pivot
            side[k] = side[k] * pivot
            for m in range(k + 1, 8):
                factor = over_rows(columns[s][k], m)
                for t in range(s, blocks):
                    columns[t][m] = columns[t][m] - columns[t][k] * factor
                upper[m] = upper[m] - upper[k] * factor
                side[m] = side[m] - side[k] * factor
            if s + 1 < blocks:
                for j in range(8):
                    factor = over_rows(columns[s + 1][k], j)
                    for t in early:
                        ready[t][j] = ready[t][j] - columns[t][k] * factor
        done = lanes < 8 * s + 8
        both = [jnp.where(done, side[k], upper[k]) for k in range(8)]
        for t in range(s + 1, blocks):
            a[t] = jnp.where((lanes < 8 * s) | (lanes >= 8 * s + 8), a[t], 0.0)
            for k in range(8):
                a[t] = a[t] - columns[t][k] * both[k]
        for k in range(1, 8):
            upper[0] = jnp.where(rows >= k, upper[k], upper[0])
            side[0] = jnp.where(rows >= k, side[k], side[0])
        a_ref[8 * s : 8 * s + 8, :] = jnp.where(lanes >= rows + 8 * s, upper[0], 0.0)
        e_ref[8 * s : 8 * s + 8, :] = side[0]


def factor_steps(work, r_ref, x_ref, tile_a, tile_e):
    size = work.shape[0]
    blocks = size // TILE
    r_ref[...] = jnp.zeros((size, size), jnp.float32)
    x_ref[...] = jnp.zeros((size, size), jnp.float32)

    def block_step(b, carry):
        spot = pl.ds(pl.multiple_of(b * TILE, TILE), TILE)
        tile_a[...] = work[spot, spot]
        factor_tile(tile_a, tile_e)
        r_ref[spot, spot] = tile_a[...]
        x_ref[spot, spot] = tile_e[...]
        for at in range(blocks):
            here, rest = slice(TILE * at, TILE * at + TILE), slice(TILE * at + TILE, size)

            @pl.when(b == at)
            def _():
                inverse = pieces(tile_e[...])
                if at > 0:
                    done = slice(0, TILE * at)
                    x_ref[here, done] = close_dot(inverse, pieces(x_ref[here, done]), PLAIN)
                if at < blocks - 1:
                    right = close_dot(inverse, pieces(work[here, rest]), PLAIN)
                    r_ref[here, rest] = right
                    right = pieces(right)
                    work[rest, rest] = work[rest, rest] - close_dot(right, right, ACROSS)
                    done = slice(0, TILE * at + TILE)
                    x_ref[rest, done] = x_ref[rest, done] - close_dot(right, pieces(x_ref[here, done]), ACROSS)

        return carry

    lax.fori_loop(0, blocks, block_step, 0)


def factor_scratch(size):
    return [pltpu.VMEM((size, size), jnp.float32)] + [pltpu.VMEM((TILE, TILE), jnp.float32)] * 2


def factor_kernel(g_ref, r_ref, x_ref, work, tile_a, tile_e):
    work[...] = g_ref[...]
    factor_steps(work, r_ref, x_ref, tile_a, tile_e)


def factorize(gram):
    size = gram.shape[0]
    square = jax.ShapeDtypeStruct((size, size), jnp.float32)
    return pl.pallas_call(
        factor_kernel,
        in_specs=[VMEM],
        out_specs=[VMEM, VMEM],
        out_shape=[square, square],
        scratch_shapes=factor_scratch(size),
        compiler_params=PARAMS,
    )(gram)


def pair_kernel(count, g_ref, r_ref, own_ref, other_ref, work, tile_a, tile_e, r_all, x_all):
    rows = r_ref.shape[0]
    share = rows // count
    work[rows:, :rows] = jnp.zeros((rows, rows), jnp.float32)
    for place in range(count):
        start = pl.multiple_of(block_at(place, count) * share, share)
        here = slice(share * place, share * place + share)
        work[pl.ds(start, share), :] = g_ref[here, : 2 * rows]
        work[pl.ds(rows + start, share), rows:] = g_ref[here, 2 * rows :]
    factor_steps(work, r_all, x_all, tile_a, tile_e)
    is_first = lax.axis_index("probe") == 0

    @pl.when(is_first)
    def _():
        r_ref[...] = r_all[:rows, :]
        own_ref[...] = x_all[:rows, :rows]
        other_ref[...] = jnp.zeros((rows, rows), jnp.float32)

    @pl.when(jnp.logical_not(is_first))
    def _():
        r_ref[...] = r_all[rows:, :]
        own_ref[...] = x_all[rows:, rows:]
        other_ref[...] = x_all[rows:, :rows]


def factorize_pair(travelled, count):
    rows = travelled.shape[0]
    square = jax.ShapeDtypeStruct((rows, rows), jnp.float32)
    return pl.pallas_call(
        functools.partial(pair_kernel, count),
        in_specs=[VMEM],
        out_specs=[VMEM] * 3,
        out_shape=[jax.ShapeDtypeStruct((rows, 2 * rows), jnp.float32), square, square],
        scratch_shapes=factor_scratch(2 * rows) + [pltpu.VMEM((2 * rows, 2 * rows), jnp.float32)] * 2,
        compiler_params=PARAMS,
        cost_estimate=taking(15),
    )(travelled)


def basis_kernel(own_ref, other_ref, outer_ref, inner_ref, front_ref, back_ref, raw_ref, ready_ref, early_ref, late_ref, out_ref):
    me = lax.axis_index("probe")
    quarter = outer_ref.shape[2]
    own = pieces(own_ref[...])
    places = (me * 3, 1 + me, (1 - me) * 2, (1 - me) * 2 + 1)
    for place, ref in zip(places, (outer_ref, inner_ref, front_ref, back_ref)):
        spot = pl.ds(pl.multiple_of(place * quarter, TILE), quarter)
        out_ref[0, :, spot] = close_dot(own, pieces(ref[0]), PLAIN)

    @pl.when(me == 1)
    def _():
        other = pieces(other_ref[...])
        for at, ref in enumerate((raw_ref, ready_ref, early_ref, late_ref)):
            spot = slice(quarter * at, quarter * at + quarter)
            out_ref[0, :, spot] = out_ref[0, :, spot] + close_dot(other, pieces(ref[0]), PLAIN)


def basis_of(own, other, *panels):
    _, rows, quarter = panels[0].shape
    weights = pl.BlockSpec((rows, rows), lambda k: (0, 0))
    panel = pl.BlockSpec((1, rows, quarter), lambda k: (k, 0, 0))
    return pl.pallas_call(
        basis_kernel,
        grid=(3,),
        in_specs=[weights] * 2 + [panel] * len(panels),
        out_specs=pl.BlockSpec((1, rows, 4 * quarter), lambda k: (k, 0, 0)),
        out_shape=jax.ShapeDtypeStruct((3, rows, 4 * quarter), jnp.float32),
        compiler_params=PARAMS,
    )(own, other, *panels)


def partners(axis, bit):
    return [(i, i ^ bit) for i in range(lax.axis_size(axis))]


def bits_of(axis):
    bits, bit = [], 1
    while bit < lax.axis_size(axis):
        bits.append(bit)
        bit *= 2
    return bits


def split_bits(axis):
    bits = bits_of(axis)
    return bits[: max(len(bits) - 2, 0)], bits[max(len(bits) - 2, 0) :]


def scatter_sum(block, axis):
    halved, whole = split_bits(axis)
    for bit in halved:
        half = block.shape[0] // 2
        block = block[:half] + lax.ppermute(block[half:], axis, partners(axis, bit))
    for bit in whole:
        block = block + lax.ppermute(block, axis, partners(axis, bit))
    return block


def gather_back(block, axis):
    for bit in reversed(split_bits(axis)[0]):
        block = jnp.concatenate([block, lax.ppermute(block, axis, partners(axis, bit))], 0)
    return block


def swapped(block):
    return lax.ppermute(block, "probe", [(0, 1), (1, 0)])


def halo_of(first, last):
    slabs = lax.axis_size("slab")
    forward = [(i, i + 1) for i in range(slabs - 1)]
    return lax.ppermute(last, "slab", forward), lax.ppermute(first, "slab", [(b, a) for a, b in forward])


def pair_body(probes, coefs, first, mid, last, offsets):
    _, columns, cells = probes.shape
    slabs = lax.axis_size("slab")
    scale = 1.0 / (3 * cells * slabs)
    me = lax.axis_index("probe")
    is_first = me == 0
    quarter = cells // 4
    tiles = quarter // TILE

    low, high = halo_of(first, last)
    pack = 3 * HALO
    ends = swapped(
        jnp.where(
            is_first,
            jnp.concatenate([low[:pack], mid[:pack]], 0),
            jnp.concatenate([mid[:pack], high[:pack]], 0),
        )
    )
    theirs = swapped(lax.dynamic_slice_in_dim(probes, me * 3 * quarter, quarter, 2))
    run = functools.partial(segment, offsets=offsets, coefs=coefs)

    def at_half(me):
        return me * 2 * tiles

    def at_other_half(me):
        return (1 - me) * 2 * tiles

    def at_raw(me):
        return (1 - me) * 3 * tiles

    edges = (low, high)
    outer, inner = run(at_half, at_half, 2 * tiles, x=probes, edges=edges, parts=2, inward=True)
    inner, ends = lax.optimization_barrier((inner, ends))
    ready = swapped(inner)
    front, back, gram = run(
        at_other_half, at_other_half, 2 * tiles, x=probes, edges=edges, parts=2, rest=(inner, outer), scale=scale
    )
    early = swapped(front)
    raw = run(lambda me: 0, at_raw, tiles, x=theirs, edges=edges, ends=ends)
    count = 1 << len(split_bits("slab")[0])
    own, cross = cross_of(front, back, raw, ready, gram, scale, count)
    own, cross = scatter_sum(own, "slab"), scatter_sum(cross, "slab")
    own, cross, early = lax.optimization_barrier((own, cross, early))
    their_own, their_cross = swapped(own), swapped(cross)
    their_own, their_cross, late = lax.optimization_barrier((their_own, their_cross, back))
    late = swapped(late)
    share = jnp.concatenate(
        [jnp.where(is_first, own, their_own), cross + their_cross, jnp.where(is_first, their_own, own)], 1
    )
    r_rows, own, other = factorize_pair(gather_back(share, "slab"), count)
    return basis_of(own, other, outer, inner, front, back, raw, ready, early, late), r_rows


def whole_body(probes, coefs, first, mid, last, offsets):
    _, columns, cells = probes.shape
    slabs = lax.axis_size("slab")
    me = lax.axis_index("probe")
    scale = 1.0 / (3 * cells * slabs)
    low, high = halo_of(first, last)
    panel = segment(lambda me: 0, lambda me: 0, cells // TILE, offsets, probes, coefs, (low, high))
    everyone = lax.all_gather(panel, "probe", axis=1, tiled=True)
    part = scale * jnp.einsum("kpc,kqc->pq", panel, everyone, precision=CLOSE)
    gram = lax.all_gather(lax.psum(part, "slab"), "probe", axis=0, tiled=True)
    upper, inverse = factorize(gram)
    mine = lax.dynamic_slice_in_dim(inverse, me * columns, columns, 0)
    basis = jnp.einsum("pq,kqc->kpc", mine, everyone, precision=CLOSE)
    return basis, lax.dynamic_slice_in_dim(upper, me * columns, columns, 0)


def body(probes, viscosity, coupling, misfit_weight, band_offsets):
    first, mid, last, coefs = pack_edges(probes, coupling, viscosity, misfit_weight)
    run = pair_body if lax.axis_size("probe") == 2 else whole_body
    return run(probes, coefs, first, mid, last, band_offsets)


def solution(mesh):
    return jax.shard_map(
        body,
        mesh=mesh,
        in_specs=(
            P(None, "probe", "slab"),
            P("slab"),
            P(None, None, None, "slab"),
            P(None, "slab"),
            P(),
        ),
        out_specs=(P(None, "probe", "slab"), P("probe", None)),
        check_vma=False,
    )
```

```python
import functools

import jax
import jax.numpy as jnp
from jax import lax
from jax.experimental import pallas as pl
from jax.experimental.pallas import tpu as pltpu
from jax.sharding import PartitionSpec as P

REACH = 4
BANDS = 4
HALO = 4 * REACH
TERMS = 9 * BANDS
COEFS = TERMS + 4
TILE = 128
EARLY = 1
AT_ONCE = 8
EXACT = lax.Precision.HIGHEST
CLOSE = lax.Precision.HIGH
VMEM = pl.BlockSpec(memory_space=pltpu.VMEM)


def taking(micros):
    return pl.CostEstimate(flops=0, transcendentals=0, bytes_accessed=int(micros * 3.5e6))


PARAMS = pltpu.CompilerParams(vmem_limit_bytes=32 * 2**20)


def pack_kernel(x_ref, *refs):
    given, (low_ref, mid_ref, high_ref, coef_ref, tiles_ref), held, sems = refs[:3], refs[3:8], refs[8:11], refs[11]
    rows, cells = x_ref.shape[1], coef_ref.shape[1]
    blank = jnp.zeros((rows - COEFS, TILE), jnp.float32)
    is_first = lax.axis_index("probe") == 0
    middle = jnp.where(is_first, cells // 4, cells // 4 * 3 - TILE)
    starts = (0, pl.multiple_of(middle, TILE), cells - TILE)
    copies = [
        pltpu.make_async_copy(x_ref.at[:, :, pl.ds(start, TILE)], tiles_ref.at[at], sems.at[at])
        for at, start in enumerate(starts)
    ]
    copies += [pltpu.make_async_copy(one, two, sems.at[3 + at]) for at, (one, two) in enumerate(zip(given, held))]
    for copy in copies:
        copy.start()
    for copy in copies:
        copy.wait()
    coup_ref, visc_ref, weight_ref = held
    for k in range(3):
        for m in range(3):
            start = BANDS * (3 * k + m)
            coef_ref[start : start + BANDS, :] = coup_ref[k, m]
    coef_ref[TERMS : TERMS + 1, :] = visc_ref[...]
    coef_ref[TERMS + 1 :, :] = weight_ref[...]

    def pack(out_ref, at, spot):
        for comp in range(3):
            out_ref[HALO * comp : HALO * comp + HALO, :] = tiles_ref[at, comp].T[spot]
        coef = jnp.concatenate([coef_ref[:, pl.ds(starts[at], TILE)], blank], 0)
        out_ref[3 * HALO : 4 * HALO, :] = coef.T[spot]

    head, tail = slice(0, HALO), slice(TILE - HALO, TILE)
    pack(low_ref, 0, head)
    pack(high_ref, 2, tail)

    @pl.when(is_first)
    def _():
        pack(mid_ref, 1, head)

    @pl.when(jnp.logical_not(is_first))
    def _():
        pack(mid_ref, 1, tail)


def pack_edges(probes, coupling, viscosity, misfit_weight):
    _, rows, cells = probes.shape
    edge = jax.ShapeDtypeStruct((4 * HALO, rows), jnp.float32)
    return pl.pallas_call(
        pack_kernel,
        in_specs=[pl.BlockSpec(memory_space=pltpu.HBM)] * 4,
        out_specs=[VMEM] * 4,
        out_shape=[edge] * 3 + [jax.ShapeDtypeStruct((COEFS, cells), jnp.float32)],
        scratch_shapes=[
            pltpu.VMEM((3, 3, rows, TILE), jnp.float32),
            pltpu.VMEM((3, 3, BANDS, cells), jnp.float32),
            pltpu.VMEM((1, cells), jnp.float32),
            pltpu.VMEM((3, cells), jnp.float32),
            pltpu.SemaphoreType.DMA((6,)),
        ],
        compiler_params=pltpu.CompilerParams(vmem_limit_bytes=60 * 2**20),
    )(probes, coupling.transpose(1, 2, 0, 3), viscosity[None, :], misfit_weight)


def turned(x, amount):
    if isinstance(amount, int):
        return pltpu.roll(x, (TILE - amount) % TILE, 1)
    return pltpu.roll(x, lax.rem(TILE - amount, TILE), 1)


def moved(tiles, amount, lane):
    turns = [turned(t, amount) for t in tiles]
    return [
        jnp.where(lane < TILE - amount, turns[i], turns[min(i + 1, len(tiles) - 1)])
        for i in range(len(tiles))
    ]


def stretch(tiles, lane):
    turns = [turned(t, TILE - HALO) for t in tiles]
    return [jnp.where(lane < HALO, turns[i], turns[i + 1]) for i in range(len(tiles) - 1)]


def segment_steps(x_at, coef_at, count, inward, off_ref, x_ref, coef_ref, edges, out_refs, scratch):
    rows = edges[0].shape[1]
    tab_ref, mid_ref, in_ref, ends_ref, here_ref, sem = scratch
    fetch = pltpu.make_async_copy(x_ref, here_ref, sem)
    fetch.start()
    lane = lax.broadcasted_iota(jnp.int32, (8, TILE), 1)
    given = [off_ref[b] for b in range(BANDS)]
    slots = [sum((other < off).astype(jnp.int32) for other in given) for off in given]
    offs = [sum(jnp.where(slot == r, off, 0) for slot, off in zip(slots, given)) for r in range(BANDS)]
    offs[0], offs[-1] = -REACH, REACH
    me = lax.axis_index("probe")
    x_first, coef_first = x_at(me), coef_at(me)

    coef_low_ref, coef_high_ref, *x_ends = edges
    blank = jnp.zeros((TILE - HALO, rows), jnp.float32)
    for comp in range(4):
        start = HALO * comp
        low, high = coef_low_ref[start : start + HALO, :], coef_high_ref[start : start + HALO, :]
        if comp < 3 and x_ends:
            low = x_ends[0][start : start + HALO, :]
            high = x_ends[0][start + 3 * HALO : start + 4 * HALO, :]
        ends_ref[comp] = jnp.concatenate([blank, low], 0).T
        ends_ref[4 + comp] = jnp.concatenate([high, blank], 0).T

    def tiles_of(load, first, total, comp, spot):
        def at(i):
            start = i * TILE
            return load(pl.ds(start if isinstance(i, int) else pl.multiple_of(start, TILE), TILE))

        def edge(is_end, which, i):
            halo = ends_ref[which + comp, spot, :]
            if isinstance(first, int):
                return halo if is_end else at(i)
            return jnp.where(is_end, halo, at(jnp.clip(i, 0, total - 1)))

        return (
            [edge(first == 0, 0, first - 1)]
            + [at(first + i) for i in range(count)]
            + [edge(first + count == total, 4, first + count)]
        )

    for group in range(COEFS // 8):
        spot = slice(8 * group, 8 * group + 8)
        coef_total = coef_ref.shape[1] // TILE
        ext = stretch(
            tiles_of(lambda where: coef_ref[spot, where], coef_first, coef_total, 3, spot), lane
        )
        by_step = {(0, b): moved(ext, REACH, lane) for b in range(BANDS)}
        by_step.update({(2, b): moved(ext, 3 * REACH, lane) for b in range(BANDS)})
        for b in range(BANDS):
            by_step[1, b] = moved(ext, 2 * REACH - given[b], lane)
            by_step[3, b] = moved(ext, 4 * REACH - given[b], lane)
        for j in range(8):
            row = 8 * group + j
            if row >= TERMS:
                continue
            for step in range(4):
                for i in range(count + 1):
                    tile = by_step[step, row % BANDS][i]
                    tab_ref[step, 9 * slots[row % BANDS] + row // BANDS, :, TILE * i : TILE * i + TILE] = jnp.broadcast_to(
                        tile[j : j + 1, :], (8, TILE)
                    )
        if group == COEFS // 8 - 1:
            for half, step in enumerate((0, 2)):
                for i in range(count + 1):
                    tile = by_step[step, 0][i]
                    visc = jnp.broadcast_to(tile[4:5, :], (8, TILE))
                    for comp in range(3):
                        weight = jnp.broadcast_to(tile[5 + comp : 6 + comp, :], (8, TILE))
                        mid_ref[half, comp, :, TILE * i : TILE * i + TILE] = visc * visc * weight
            between = moved(ext, 2 * REACH, lane)
            for at, i in enumerate((0, count)):
                inside = jnp.broadcast_to(between[i][4:5, :], (8, TILE)) != 0.0
                in_ref[at] = jnp.where(inside, 1.0, 0.0)

    def apply(tiles, step, outs):
        sign = 1 if step % 2 == 0 else -1
        result = [[[], [], []] for _ in range(AT_ONCE)]
        amounts = [REACH] + [REACH + sign * off for off in offs]
        masks = [lane < TILE - amount for amount in amounts]

        def turns_of(i):
            return [
                [
                    [row[i] if isinstance(amount, int) and amount == 0 else turned(row[i], amount) for amount in amounts]
                    for row in tiles[at]
                ]
                for at in range(AT_ONCE)
            ]

        ahead = turns_of(0)
        for i in range(outs):
            here = ahead
            ahead = turns_of(i + 1) if i + 1 < len(tiles[0][0]) else here
            spot = slice(TILE * i, TILE * i + TILE)
            shifted = [
                [
                    [
                        here[at][m][j]
                        if isinstance(amounts[j], int) and amounts[j] == 0
                        else jnp.where(masks[j], here[at][m][j], ahead[at][m][j])
                        for j in range(1 + BANDS)
                    ]
                    for m in range(3)
                ]
                for at in range(AT_ONCE)
            ]

            def sums(k):
                total = [shifted[at][k][0] for at in range(AT_ONCE)]
                for b in range(BANDS):
                    for m in range(3):
                        term = 9 * b + (3 * k + m if sign == 1 else 3 * m + k)
                        table = tab_ref[step, term, :, spot]
                        total = [total[at] + table * shifted[at][m][1 + b] for at in range(AT_ONCE)]
                return total

            for k in range(3):
                total = sums(k)
                if step % 2 == 0:
                    middle = mid_ref[step // 2, k, :, spot]
                    total = [x * middle for x in total]
                if step == 1 and i in (0, count):
                    inside = in_ref[0 if i == 0 else 1]
                    total = [x * inside for x in total]
                for at in range(AT_ONCE):
                    result[at][k].append(total[at])
        return result

    def group_step(g, carry):
        spots = [pl.ds(pl.multiple_of(8 * (AT_ONCE * g + at), 8), 8) for at in range(AT_ONCE)]
        total = x_ref.shape[-1] // TILE

        def load(m, at, where):
            return here_ref[m, spots[at], where]

        tiles = [
            [
                stretch(
                    tiles_of(functools.partial(load, m, at), x_first, total, m, spot), lane
                )
                for m in range(3)
            ]
            for at, spot in enumerate(spots)
        ]
        for step in range(4):
            tiles = apply(tiles, step, count + 1 if step < 3 else count)
        for at, spot in enumerate(spots):
            for m in range(3):
                for i in range(count // len(out_refs)):
                    here = slice(TILE * i, TILE * i + TILE)
                    if len(out_refs) == 1:
                        out_refs[0][m, spot, here] = tiles[at][m][i]
                    else:
                        one, two = tiles[at][m][i], tiles[at][m][count // 2 + i]
                        if inward:
                            one, two = jnp.where(me == 0, one, two), jnp.where(me == 0, two, one)
                        out_refs[0][m, spot, here] = one
                        out_refs[1][m, spot, here] = two
        return carry

    fetch.wait()
    lax.fori_loop(0, rows // (8 * AT_ONCE), group_step, 0)


def segment_scratch(rows, count):
    wide = (count + 1) * TILE
    return [
        pltpu.VMEM((4, TERMS, 8, wide), jnp.float32),
        pltpu.VMEM((2, 3, 8, wide), jnp.float32),
        pltpu.VMEM((2, 8, TILE), jnp.float32),
        pltpu.VMEM((8, rows, TILE), jnp.float32),
    ]


SMEM = pl.BlockSpec(memory_space=pltpu.SMEM)


def pieces(x):
    high = x.astype(jnp.bfloat16)
    return high, (x - high.astype(jnp.float32)).astype(jnp.bfloat16)


def close_dot(left, right, over):
    left = jnp.concatenate([left[0], left[0], left[1]], over[0][0])
    right = jnp.concatenate([right[0], right[1], right[0]], over[1][0])
    return lax.dot_general(left, right, (over, ((), ())), preferred_element_type=jnp.float32)


ALONG = ((1,), (1,))
PLAIN = ((1,), (0,))
ACROSS = ((0,), (0,))


def joined(refs, k):
    return pieces(jnp.concatenate([ref[k] for ref in refs], 1))


def products(left, right):
    total = None
    for k in range(3):
        part = close_dot(joined(left, k), joined(right, k), ALONG)
        total = part if total is None else total + part
    return total


def own_products(refs):
    dot = functools.partial(lax.dot_general, dimension_numbers=(ALONG, ((), ())), preferred_element_type=jnp.float32)
    main = mixed = None
    for k in range(3):
        high, low = joined(refs, k)
        one, two = dot(high, high), dot(high, low)
        main, mixed = (one, two) if main is None else (main + one, mixed + two)
    return main + (mixed + mixed.T)


def segment_kernel(x_at, coef_at, count, parts, inward, scale, bounds, off_ref, x_ref, coef_ref, *refs):
    edges, refs = refs[:bounds], refs[bounds:]
    rest, refs = (refs[:2], refs[2:]) if scale else ((), refs)
    out_refs, refs = refs[:parts], refs[parts:]
    gram_ref, refs = (refs[0], refs[1:]) if scale else (None, refs)
    segment_steps(x_at, coef_at, count, inward, off_ref, x_ref, coef_ref, edges, out_refs, refs)
    if scale:
        gram_ref[...] = own_products((*out_refs, *rest)) * scale


def segment(x_at, coef_at, count, offsets, x, coefs, edges, ends=None, parts=1, inward=False, rest=(), scale=None):
    rows = edges[0].shape[1]
    scratch = segment_scratch(rows, count) + [pltpu.VMEM(x.shape, jnp.float32), pltpu.SemaphoreType.DMA(())]
    if ends is not None:
        edges = (*edges, ends)
    shapes = [jax.ShapeDtypeStruct((3, rows, count * TILE // parts), jnp.float32)] * parts
    if scale:
        shapes.append(jax.ShapeDtypeStruct((rows, rows), jnp.float32))
    result = pl.pallas_call(
        functools.partial(segment_kernel, x_at, coef_at, count, parts, inward, scale, len(edges)),
        in_specs=[SMEM, pl.BlockSpec(memory_space=pltpu.HBM)] + [VMEM] * (1 + len(edges) + len(rest)),
        out_specs=[VMEM] * len(shapes),
        out_shape=shapes,
        scratch_shapes=scratch,
        compiler_params=PARAMS,
        cost_estimate=taking(2 + 2 * (count + 1) * rows / 256),
    )(offsets, x, coefs, *edges, *rest)
    return result if len(shapes) > 1 else result[0]


def reversed_bits(place, count):
    result, bit = 0, 1
    while bit < count:
        result = 2 * result + (place // bit) % 2
        bit *= 2
    return result


def block_at(place, count):
    return lax.bitwise_xor(lax.rem(lax.axis_index("slab"), count), jnp.int32(reversed_bits(place, count)))


def cross_kernel(scale, count, front_ref, back_ref, raw_ref, ready_ref, gram_ref, own_ref, out_ref, work):
    rows = gram_ref.shape[0]
    is_first = lax.axis_index("probe") == 0

    @pl.when(is_first)
    def _():
        work[...] = products((front_ref, back_ref), (ready_ref, raw_ref)) * scale

    @pl.when(jnp.logical_not(is_first))
    def _():
        work[...] = products((raw_ref, ready_ref), (front_ref, back_ref)) * scale

    share = rows // count
    for place in range(count):
        spot = pl.ds(pl.multiple_of(block_at(place, count) * share, share), share)
        own_ref[share * place : share * place + share, :] = gram_ref[spot, :]
        out_ref[share * place : share * place + share, :] = work[spot, :]


def cross_of(front, back, raw, ready, gram, scale, count):
    rows = gram.shape[0]
    return pl.pallas_call(
        functools.partial(cross_kernel, scale, count),
        in_specs=[VMEM] * 5,
        out_specs=[VMEM] * 2,
        out_shape=[jax.ShapeDtypeStruct((rows, rows), jnp.float32)] * 2,
        scratch_shapes=[pltpu.VMEM((rows, rows), jnp.float32)],
        compiler_params=PARAMS,
    )(front, back, raw, ready, gram)


def over_lanes(x, j):
    return jnp.broadcast_to(x[:, j : j + 1], (8, TILE))


def over_rows(x, i):
    return jnp.broadcast_to(x[i : i + 1, :], (8, TILE))


def factor_tile(a_ref, e_ref):
    blocks = TILE // 8
    rows = lax.broadcasted_iota(jnp.int32, (8, TILE), 0)
    lanes = lax.broadcasted_iota(jnp.int32, (8, TILE), 1)
    a = [a_ref[8 * t : 8 * t + 8, :] for t in range(blocks)]

    def repeated(t, s):
        return [over_lanes(a[t], 8 * s + j) for j in range(8)]

    ready = {}
    for s in range(blocks):
        columns = {t: ready[t] if t in ready else repeated(t, s) for t in range(s, blocks)}
        early = range(s + 1, min(s + 1 + EARLY, blocks))
        ready = {t: repeated(t, s + 1) for t in early}
        upper = [over_rows(a[s], k) for k in range(8)]
        side = [jnp.where(lanes < 8 * s, upper[k], jnp.where(lanes == 8 * s + k, 1.0, 0.0)) for k in range(8)]
        for k in range(8):
            pivot = lax.rsqrt(over_rows(columns[s][k], k))
            for t in range(s, blocks):
                columns[t][k] = columns[t][k] * pivot
            upper[k] = upper[k] * pivot
            side[k] = side[k] * pivot
            for m in range(k + 1, 8):
                factor = over_rows(columns[s][k], m)
                for t in range(s, blocks):
                    columns[t][m] = columns[t][m] - columns[t][k] * factor
                upper[m] = upper[m] - upper[k] * factor
                side[m] = side[m] - side[k] * factor
            if s + 1 < blocks:
                for j in range(8):
                    factor = over_rows(columns[s + 1][k], j)
                    for t in early:
                        ready[t][j] = ready[t][j] - columns[t][k] * factor
        done = lanes < 8 * s + 8
        both = [jnp.where(done, side[k], upper[k]) for k in range(8)]
        for t in range(s + 1, blocks):
            a[t] = jnp.where((lanes < 8 * s) | (lanes >= 8 * s + 8), a[t], 0.0)
            for k in range(8):
                a[t] = a[t] - columns[t][k] * both[k]
        for k in range(1, 8):
            upper[0] = jnp.where(rows >= k, upper[k], upper[0])
            side[0] = jnp.where(rows >= k, side[k], side[0])
        a_ref[8 * s : 8 * s + 8, :] = jnp.where(lanes >= rows + 8 * s, upper[0], 0.0)
        e_ref[8 * s : 8 * s + 8, :] = side[0]


def factor_steps(work, r_ref, x_ref, tile_a, tile_e):
    size = work.shape[0]
    blocks = size // TILE
    r_ref[...] = jnp.zeros((size, size), jnp.float32)
    x_ref[...] = jnp.zeros((size, size), jnp.float32)

    def block_step(b, carry):
        spot = pl.ds(pl.multiple_of(b * TILE, TILE), TILE)
        tile_a[...] = work[spot, spot]
        factor_tile(tile_a, tile_e)
        r_ref[spot, spot] = tile_a[...]
        x_ref[spot, spot] = tile_e[...]
        for at in range(blocks):
            here, rest = slice(TILE * at, TILE * at + TILE), slice(TILE * at + TILE, size)

            @pl.when(b == at)
            def _():
                inverse = pieces(tile_e[...])
                if at > 0:
                    done = slice(0, TILE * at)
                    x_ref[here, done] = close_dot(inverse, pieces(x_ref[here, done]), PLAIN)
                if at < blocks - 1:
                    right = close_dot(inverse, pieces(work[here, rest]), PLAIN)
                    r_ref[here, rest] = right
                    right = pieces(right)
                    work[rest, rest] = work[rest, rest] - close_dot(right, right, ACROSS)
                    done = slice(0, TILE * at + TILE)
                    x_ref[rest, done] = x_ref[rest, done] - close_dot(right, pieces(x_ref[here, done]), ACROSS)

        return carry

    lax.fori_loop(0, blocks, block_step, 0)


def factor_scratch(size):
    return [pltpu.VMEM((size, size), jnp.float32)] + [pltpu.VMEM((TILE, TILE), jnp.float32)] * 2


def factor_kernel(g_ref, r_ref, x_ref, work, tile_a, tile_e):
    work[...] = g_ref[...]
    factor_steps(work, r_ref, x_ref, tile_a, tile_e)


def factorize(gram):
    size = gram.shape[0]
    square = jax.ShapeDtypeStruct((size, size), jnp.float32)
    return pl.pallas_call(
        factor_kernel,
        in_specs=[VMEM],
        out_specs=[VMEM, VMEM],
        out_shape=[square, square],
        scratch_shapes=factor_scratch(size),
        compiler_params=PARAMS,
    )(gram)


def pair_kernel(count, g_ref, r_ref, own_ref, other_ref, work, tile_a, tile_e, r_all, x_all):
    rows = r_ref.shape[0]
    share = rows // count
    work[rows:, :rows] = jnp.zeros((rows, rows), jnp.float32)
    for place in range(count):
        start = pl.multiple_of(block_at(place, count) * share, share)
        here = slice(share * place, share * place + share)
        work[pl.ds(start, share), :] = g_ref[here, : 2 * rows]
        work[pl.ds(rows + start, share), rows:] = g_ref[here, 2 * rows :]
    factor_steps(work, r_all, x_all, tile_a, tile_e)
    is_first = lax.axis_index("probe") == 0

    @pl.when(is_first)
    def _():
        r_ref[...] = r_all[:rows, :]
        own_ref[...] = x_all[:rows, :rows]
        other_ref[...] = jnp.zeros((rows, rows), jnp.float32)

    @pl.when(jnp.logical_not(is_first))
    def _():
        r_ref[...] = r_all[rows:, :]
        own_ref[...] = x_all[rows:, rows:]
        other_ref[...] = x_all[rows:, :rows]


def factorize_pair(travelled, count):
    rows = travelled.shape[0]
    square = jax.ShapeDtypeStruct((rows, rows), jnp.float32)
    return pl.pallas_call(
        functools.partial(pair_kernel, count),
        in_specs=[VMEM],
        out_specs=[VMEM] * 3,
        out_shape=[jax.ShapeDtypeStruct((rows, 2 * rows), jnp.float32), square, square],
        scratch_shapes=factor_scratch(2 * rows) + [pltpu.VMEM((2 * rows, 2 * rows), jnp.float32)] * 2,
        compiler_params=PARAMS,
        cost_estimate=taking(15),
    )(travelled)


def basis_kernel(own_ref, other_ref, *refs):
    own_panels, their_panels, (out_ref, held_ref, sems) = refs[:4], refs[4:8], refs[8:]
    me = lax.axis_index("probe")
    quarter = own_panels[0].shape[2]
    own, other = pieces(own_ref[...]), pieces(other_ref[...])
    places = (me * 3, 1 + me, (1 - me) * 2, (1 - me) * 2 + 1)
    copies = [pltpu.make_async_copy(held_ref.at[k], out_ref.at[k], sems.at[k]) for k in range(3)]
    for k in range(3):
        for place, ref in zip(places, own_panels):
            spot = pl.ds(pl.multiple_of(place * quarter, TILE), quarter)
            held_ref[k, :, spot] = close_dot(own, pieces(ref[k]), PLAIN)

        @pl.when(me == 1)
        def _():
            for at, ref in enumerate(their_panels):
                spot = slice(quarter * at, quarter * at + quarter)
                held_ref[k, :, spot] = held_ref[k, :, spot] + close_dot(other, pieces(ref[k]), PLAIN)

        copies[k].start()
    for copy in copies:
        copy.wait()


def basis_of(own, other, *panels):
    _, rows, quarter = panels[0].shape
    shape = (3, rows, 4 * quarter)
    return pl.pallas_call(
        basis_kernel,
        in_specs=[VMEM] * (2 + len(panels)),
        out_specs=pl.BlockSpec(memory_space=pltpu.HBM),
        out_shape=jax.ShapeDtypeStruct(shape, jnp.float32),
        scratch_shapes=[pltpu.VMEM(shape, jnp.float32), pltpu.SemaphoreType.DMA((3,))],
        compiler_params=pltpu.CompilerParams(vmem_limit_bytes=24 * 2**20),
    )(own, other, *panels)


def partners(axis, bit):
    return [(i, i ^ bit) for i in range(lax.axis_size(axis))]


def bits_of(axis):
    bits, bit = [], 1
    while bit < lax.axis_size(axis):
        bits.append(bit)
        bit *= 2
    return bits


def split_bits(axis):
    bits = bits_of(axis)
    return bits[: max(len(bits) - 2, 0)], bits[max(len(bits) - 2, 0) :]


def scatter_sum(block, axis):
    halved, whole = split_bits(axis)
    for bit in halved:
        half = block.shape[0] // 2
        block = block[:half] + lax.ppermute(block[half:], axis, partners(axis, bit))
    for bit in whole:
        block = block + lax.ppermute(block, axis, partners(axis, bit))
    return block


def gather_back(block, axis):
    for bit in reversed(split_bits(axis)[0]):
        block = jnp.concatenate([block, lax.ppermute(block, axis, partners(axis, bit))], 0)
    return block


def swapped(block):
    return lax.ppermute(block, "probe", [(0, 1), (1, 0)])


def halo_of(first, last):
    slabs = lax.axis_size("slab")
    forward = [(i, i + 1) for i in range(slabs - 1)]
    return lax.ppermute(last, "slab", forward), lax.ppermute(first, "slab", [(b, a) for a, b in forward])


def pair_body(probes, coefs, first, mid, last, offsets):
    _, columns, cells = probes.shape
    slabs = lax.axis_size("slab")
    scale = 1.0 / (3 * cells * slabs)
    me = lax.axis_index("probe")
    is_first = me == 0
    quarter = cells // 4
    tiles = quarter // TILE

    low, high = halo_of(first, last)
    pack = 3 * HALO
    ends = swapped(
        jnp.where(
            is_first,
            jnp.concatenate([low[:pack], mid[:pack]], 0),
            jnp.concatenate([mid[:pack], high[:pack]], 0),
        )
    )
    theirs = swapped(lax.dynamic_slice_in_dim(probes, me * 3 * quarter, quarter, 2))
    run = functools.partial(segment, offsets=offsets, coefs=coefs)

    def at_half(me):
        return me * 2 * tiles

    def at_other_half(me):
        return (1 - me) * 2 * tiles

    def at_raw(me):
        return (1 - me) * 3 * tiles

    edges = (low, high)
    outer, inner = run(at_half, at_half, 2 * tiles, x=probes, edges=edges, parts=2, inward=True)
    inner, ends = lax.optimization_barrier((inner, ends))
    ready = swapped(inner)
    front, back, gram = run(
        at_other_half, at_other_half, 2 * tiles, x=probes, edges=edges, parts=2, rest=(inner, outer), scale=scale
    )
    early = swapped(front)
    raw = run(lambda me: 0, at_raw, tiles, x=theirs, edges=edges, ends=ends)
    count = 1 << len(split_bits("slab")[0])
    own, cross = cross_of(front, back, raw, ready, gram, scale, count)
    own, cross = scatter_sum(own, "slab"), scatter_sum(cross, "slab")
    own, cross, early = lax.optimization_barrier((own, cross, early))
    their_own, their_cross = swapped(own), swapped(cross)
    their_own, their_cross, late = lax.optimization_barrier((their_own, their_cross, back))
    late = swapped(late)
    share = jnp.concatenate(
        [jnp.where(is_first, own, their_own), cross + their_cross, jnp.where(is_first, their_own, own)], 1
    )
    r_rows, own, other = factorize_pair(gather_back(share, "slab"), count)
    return basis_of(own, other, outer, inner, front, back, raw, ready, early, late), r_rows


def whole_body(probes, coefs, first, mid, last, offsets):
    _, columns, cells = probes.shape
    slabs = lax.axis_size("slab")
    me = lax.axis_index("probe")
    scale = 1.0 / (3 * cells * slabs)
    low, high = halo_of(first, last)
    panel = segment(lambda me: 0, lambda me: 0, cells // TILE, offsets, probes, coefs, (low, high))
    everyone = lax.all_gather(panel, "probe", axis=1, tiled=True)
    part = scale * jnp.einsum("kpc,kqc->pq", panel, everyone, precision=CLOSE)
    gram = lax.all_gather(lax.psum(part, "slab"), "probe", axis=0, tiled=True)
    upper, inverse = factorize(gram)
    mine = lax.dynamic_slice_in_dim(inverse, me * columns, columns, 0)
    basis = jnp.einsum("pq,kqc->kpc", mine, everyone, precision=CLOSE)
    return basis, lax.dynamic_slice_in_dim(upper, me * columns, columns, 0)


def body(probes, viscosity, coupling, misfit_weight, band_offsets):
    first, mid, last, coefs = pack_edges(probes, coupling, viscosity, misfit_weight)
    run = pair_body if lax.axis_size("probe") == 2 else whole_body
    return run(probes, coefs, first, mid, last, band_offsets)


def solution(mesh):
    return jax.shard_map(
        body,
        mesh=mesh,
        in_specs=(
            P(None, "probe", "slab"),
            P("slab"),
            P(None, None, None, "slab"),
            P(None, "slab"),
            P(),
        ),
        out_specs=(P(None, "probe", "slab"), P("probe", None)),
        check_vma=False,
    )
```

```python
import functools

import jax
import jax.numpy as jnp
from jax import lax
from jax.experimental import pallas as pl
from jax.experimental.pallas import tpu as pltpu
from jax.sharding import PartitionSpec as P

REACH = 4
BANDS = 4
HALO = 4 * REACH
TERMS = 9 * BANDS
COEFS = TERMS + 4
TILE = 128
EARLY = 1
AT_ONCE = 8
EXACT = lax.Precision.HIGHEST
CLOSE = lax.Precision.HIGH
VMEM = pl.BlockSpec(memory_space=pltpu.VMEM)


def taking(micros):
    return pl.CostEstimate(flops=0, transcendentals=0, bytes_accessed=int(micros * 3.5e6))


PARAMS = pltpu.CompilerParams(vmem_limit_bytes=32 * 2**20)


def pack_kernel(x_ref, *refs):
    given, (low_ref, mid_ref, high_ref, coef_ref, tiles_ref), held, sems = refs[:3], refs[3:8], refs[8:11], refs[11]
    rows, cells = x_ref.shape[1], coef_ref.shape[1]
    blank = jnp.zeros((rows - COEFS, TILE), jnp.float32)
    is_first = lax.axis_index("probe") == 0
    middle = jnp.where(is_first, cells // 4, cells // 4 * 3 - TILE)
    starts = (0, pl.multiple_of(middle, TILE), cells - TILE)
    copies = [
        pltpu.make_async_copy(x_ref.at[:, :, pl.ds(start, TILE)], tiles_ref.at[at], sems.at[at])
        for at, start in enumerate(starts)
    ]
    copies += [pltpu.make_async_copy(one, two, sems.at[3 + at]) for at, (one, two) in enumerate(zip(given, held))]
    for copy in copies:
        copy.start()
    for copy in copies:
        copy.wait()
    coup_ref, visc_ref, weight_ref = held
    for k in range(3):
        for m in range(3):
            start = BANDS * (3 * k + m)
            coef_ref[start : start + BANDS, :] = coup_ref[k, m]
    coef_ref[TERMS : TERMS + 1, :] = visc_ref[...]
    coef_ref[TERMS + 1 :, :] = weight_ref[...]

    def pack(out_ref, at, spot):
        for comp in range(3):
            out_ref[HALO * comp : HALO * comp + HALO, :] = tiles_ref[at, comp].T[spot]
        coef = jnp.concatenate([coef_ref[:, pl.ds(starts[at], TILE)], blank], 0)
        out_ref[3 * HALO : 4 * HALO, :] = coef.T[spot]

    head, tail = slice(0, HALO), slice(TILE - HALO, TILE)
    pack(low_ref, 0, head)
    pack(high_ref, 2, tail)

    @pl.when(is_first)
    def _():
        pack(mid_ref, 1, head)

    @pl.when(jnp.logical_not(is_first))
    def _():
        pack(mid_ref, 1, tail)


def pack_edges(probes, coupling, viscosity, misfit_weight):
    _, rows, cells = probes.shape
    edge = jax.ShapeDtypeStruct((4 * HALO, rows), jnp.float32)
    return pl.pallas_call(
        pack_kernel,
        in_specs=[pl.BlockSpec(memory_space=pltpu.HBM)] * 4,
        out_specs=[VMEM] * 4,
        out_shape=[edge] * 3 + [jax.ShapeDtypeStruct((COEFS, cells), jnp.float32)],
        scratch_shapes=[
            pltpu.VMEM((3, 3, rows, TILE), jnp.float32),
            pltpu.VMEM((3, 3, BANDS, cells), jnp.float32),
            pltpu.VMEM((1, cells), jnp.float32),
            pltpu.VMEM((3, cells), jnp.float32),
            pltpu.SemaphoreType.DMA((6,)),
        ],
        compiler_params=pltpu.CompilerParams(vmem_limit_bytes=60 * 2**20),
    )(probes, coupling.transpose(1, 2, 0, 3), viscosity[None, :], misfit_weight)


def turned(x, amount):
    if isinstance(amount, int):
        return pltpu.roll(x, (TILE - amount) % TILE, 1)
    return pltpu.roll(x, lax.rem(TILE - amount, TILE), 1)


def moved(tiles, amount, lane):
    turns = [turned(t, amount) for t in tiles]
    return [
        jnp.where(lane < TILE - amount, turns[i], turns[min(i + 1, len(tiles) - 1)])
        for i in range(len(tiles))
    ]


def stretch(tiles, lane):
    turns = [turned(t, TILE - HALO) for t in tiles]
    return [jnp.where(lane < HALO, turns[i], turns[i + 1]) for i in range(len(tiles) - 1)]


def segment_steps(x_at, coef_at, count, inward, off_ref, x_ref, coef_ref, edges, out_refs, scratch):
    rows = edges[0].shape[1]
    tab_ref, mid_ref, in_ref, ends_ref, here_ref, sem = scratch
    fetch = pltpu.make_async_copy(x_ref, here_ref, sem)
    fetch.start()
    lane = lax.broadcasted_iota(jnp.int32, (8, TILE), 1)
    given = [off_ref[b] for b in range(BANDS)]
    slots = [sum((other < off).astype(jnp.int32) for other in given) for off in given]
    offs = [sum(jnp.where(slot == r, off, 0) for slot, off in zip(slots, given)) for r in range(BANDS)]
    offs[0], offs[-1] = -REACH, REACH
    me = lax.axis_index("probe")
    x_first, coef_first = x_at(me), coef_at(me)

    coef_low_ref, coef_high_ref, *x_ends = edges
    blank = jnp.zeros((TILE - HALO, rows), jnp.float32)
    for comp in range(4):
        start = HALO * comp
        low, high = coef_low_ref[start : start + HALO, :], coef_high_ref[start : start + HALO, :]
        if comp < 3 and x_ends:
            low = x_ends[0][start : start + HALO, :]
            high = x_ends[0][start + 3 * HALO : start + 4 * HALO, :]
        ends_ref[comp] = jnp.concatenate([blank, low], 0).T
        ends_ref[4 + comp] = jnp.concatenate([high, blank], 0).T

    def tiles_of(load, first, total, comp, spot):
        def at(i):
            start = i * TILE
            return load(pl.ds(start if isinstance(i, int) else pl.multiple_of(start, TILE), TILE))

        def edge(is_end, which, i):
            halo = ends_ref[which + comp, spot, :]
            if isinstance(first, int):
                return halo if is_end else at(i)
            return jnp.where(is_end, halo, at(jnp.clip(i, 0, total - 1)))

        return (
            [edge(first == 0, 0, first - 1)]
            + [at(first + i) for i in range(count)]
            + [edge(first + count == total, 4, first + count)]
        )

    for group in range(COEFS // 8):
        spot = slice(8 * group, 8 * group + 8)
        coef_total = coef_ref.shape[1] // TILE
        ext = stretch(
            tiles_of(lambda where: coef_ref[spot, where], coef_first, coef_total, 3, spot), lane
        )
        by_step = {(0, b): moved(ext, REACH, lane) for b in range(BANDS)}
        by_step.update({(2, b): moved(ext, 3 * REACH, lane) for b in range(BANDS)})
        for b in range(BANDS):
            by_step[1, b] = moved(ext, 2 * REACH - given[b], lane)
            by_step[3, b] = moved(ext, 4 * REACH - given[b], lane)
        for j in range(8):
            row = 8 * group + j
            if row >= TERMS:
                continue
            for step in range(4):
                for i in range(count + 1):
                    tile = by_step[step, row % BANDS][i]
                    tab_ref[step, 9 * slots[row % BANDS] + row // BANDS, :, TILE * i : TILE * i + TILE] = jnp.broadcast_to(
                        tile[j : j + 1, :], (8, TILE)
                    )
        if group == COEFS // 8 - 1:
            for half, step in enumerate((0, 2)):
                for i in range(count + 1):
                    tile = by_step[step, 0][i]
                    visc = jnp.broadcast_to(tile[4:5, :], (8, TILE))
                    for comp in range(3):
                        weight = jnp.broadcast_to(tile[5 + comp : 6 + comp, :], (8, TILE))
                        mid_ref[half, comp, :, TILE * i : TILE * i + TILE] = visc * visc * weight
            between = moved(ext, 2 * REACH, lane)
            for at, i in enumerate((0, count)):
                inside = jnp.broadcast_to(between[i][4:5, :], (8, TILE)) != 0.0
                in_ref[at] = jnp.where(inside, 1.0, 0.0)

    def apply(tiles, step, outs):
        sign = 1 if step % 2 == 0 else -1
        result = [[[], [], []] for _ in range(AT_ONCE)]
        amounts = [REACH] + [REACH + sign * off for off in offs]
        masks = [lane < TILE - amount for amount in amounts]

        def turns_of(i):
            return [
                [
                    [row[i] if isinstance(amount, int) and amount == 0 else turned(row[i], amount) for amount in amounts]
                    for row in tiles[at]
                ]
                for at in range(AT_ONCE)
            ]

        ahead = turns_of(0)
        for i in range(outs):
            here = ahead
            ahead = turns_of(i + 1) if i + 1 < len(tiles[0][0]) else here
            spot = slice(TILE * i, TILE * i + TILE)
            shifted = [
                [
                    [
                        here[at][m][j]
                        if isinstance(amounts[j], int) and amounts[j] == 0
                        else jnp.where(masks[j], here[at][m][j], ahead[at][m][j])
                        for j in range(1 + BANDS)
                    ]
                    for m in range(3)
                ]
                for at in range(AT_ONCE)
            ]

            def sums(k):
                total = [shifted[at][k][0] for at in range(AT_ONCE)]
                for b in range(BANDS):
                    for m in range(3):
                        term = 9 * b + (3 * k + m if sign == 1 else 3 * m + k)
                        table = tab_ref[step, term, :, spot]
                        total = [total[at] + table * shifted[at][m][1 + b] for at in range(AT_ONCE)]
                return total

            for k in range(3):
                total = sums(k)
                if step % 2 == 0:
                    middle = mid_ref[step // 2, k, :, spot]
                    total = [x * middle for x in total]
                if step == 1 and i in (0, count):
                    inside = in_ref[0 if i == 0 else 1]
                    total = [x * inside for x in total]
                for at in range(AT_ONCE):
                    result[at][k].append(total[at])
        return result

    def group_step(g, carry):
        spots = [pl.ds(pl.multiple_of(8 * (AT_ONCE * g + at), 8), 8) for at in range(AT_ONCE)]
        total = x_ref.shape[-1] // TILE

        def load(m, at, where):
            return here_ref[m, spots[at], where]

        tiles = [
            [
                stretch(
                    tiles_of(functools.partial(load, m, at), x_first, total, m, spot), lane
                )
                for m in range(3)
            ]
            for at, spot in enumerate(spots)
        ]
        for step in range(4):
            tiles = apply(tiles, step, count + 1 if step < 3 else count)
        for at, spot in enumerate(spots):
            for m in range(3):
                for i in range(count // len(out_refs)):
                    here = slice(TILE * i, TILE * i + TILE)
                    if len(out_refs) == 1:
                        out_refs[0][m, spot, here] = tiles[at][m][i]
                    else:
                        one, two = tiles[at][m][i], tiles[at][m][count // 2 + i]
                        if inward:
                            one, two = jnp.where(me == 0, one, two), jnp.where(me == 0, two, one)
                        out_refs[0][m, spot, here] = one
                        out_refs[1][m, spot, here] = two
        return carry

    fetch.wait()
    lax.fori_loop(0, rows // (8 * AT_ONCE), group_step, 0)


def segment_scratch(rows, count):
    wide = (count + 1) * TILE
    return [
        pltpu.VMEM((4, TERMS, 8, wide), jnp.float32),
        pltpu.VMEM((2, 3, 8, wide), jnp.float32),
        pltpu.VMEM((2, 8, TILE), jnp.float32),
        pltpu.VMEM((8, rows, TILE), jnp.float32),
    ]


SMEM = pl.BlockSpec(memory_space=pltpu.SMEM)


def pieces(x):
    high = x.astype(jnp.bfloat16)
    return high, (x - high.astype(jnp.float32)).astype(jnp.bfloat16)


def close_dot(left, right, over):
    left = jnp.concatenate([left[0], left[0], left[1]], over[0][0])
    right = jnp.concatenate([right[0], right[1], right[0]], over[1][0])
    return lax.dot_general(left, right, (over, ((), ())), preferred_element_type=jnp.float32)


ALONG = ((1,), (1,))
PLAIN = ((1,), (0,))
ACROSS = ((0,), (0,))


def joined(refs, k):
    return pieces(jnp.concatenate([ref[k] for ref in refs], 1))


def products(left, right):
    total = None
    for k in range(3):
        part = close_dot(joined(left, k), joined(right, k), ALONG)
        total = part if total is None else total + part
    return total


def own_products(refs):
    dot = functools.partial(lax.dot_general, dimension_numbers=(ALONG, ((), ())), preferred_element_type=jnp.float32)
    main = mixed = None
    for k in range(3):
        high, low = joined(refs, k)
        one, two = dot(high, high), dot(high, low)
        main, mixed = (one, two) if main is None else (main + one, mixed + two)
    return main + (mixed + mixed.T)


def segment_kernel(x_at, coef_at, count, parts, inward, scale, bounds, off_ref, x_ref, coef_ref, *refs):
    edges, refs = refs[:bounds], refs[bounds:]
    rest, refs = (refs[:2], refs[2:]) if scale else ((), refs)
    out_refs, refs = refs[:parts], refs[parts:]
    gram_ref, work, refs = (refs[0], refs[-1], refs[1:-1]) if scale else (None, None, refs)
    segment_steps(x_at, coef_at, count, inward, off_ref, x_ref, coef_ref, edges, out_refs, refs)
    if scale:
        work[...] = own_products((*out_refs, *rest)) * scale
        in_travelling_order(work, gram_ref)


def segment(x_at, coef_at, count, offsets, x, coefs, edges, ends=None, parts=1, inward=False, rest=(), scale=None):
    rows = edges[0].shape[1]
    scratch = segment_scratch(rows, count) + [pltpu.VMEM(x.shape, jnp.float32), pltpu.SemaphoreType.DMA(())]
    if ends is not None:
        edges = (*edges, ends)
    shapes = [jax.ShapeDtypeStruct((3, rows, count * TILE // parts), jnp.float32)] * parts
    if scale:
        shapes.append(jax.ShapeDtypeStruct((rows, rows), jnp.float32))
        scratch.append(pltpu.VMEM((rows, rows), jnp.float32))
    result = pl.pallas_call(
        functools.partial(segment_kernel, x_at, coef_at, count, parts, inward, scale, len(edges)),
        in_specs=[SMEM, pl.BlockSpec(memory_space=pltpu.HBM)] + [VMEM] * (1 + len(edges) + len(rest)),
        out_specs=[VMEM] * len(shapes),
        out_shape=shapes,
        scratch_shapes=scratch,
        compiler_params=PARAMS,
        cost_estimate=taking(2 + 2 * (count + 1) * rows / 256),
    )(offsets, x, coefs, *edges, *rest)
    return result if len(shapes) > 1 else result[0]


def reversed_bits(place, count):
    result, bit = 0, 1
    while bit < count:
        result = 2 * result + (place // bit) % 2
        bit *= 2
    return result


def block_at(place, count):
    return lax.bitwise_xor(lax.rem(lax.axis_index("slab"), count), jnp.int32(reversed_bits(place, count)))


def in_travelling_order(work, out_ref):
    rows = work.shape[0]
    count = 1 << len(split_bits("slab")[0])
    share = rows // count
    for place in range(count):
        spot = pl.ds(pl.multiple_of(block_at(place, count) * share, share), share)
        out_ref[share * place : share * place + share, :] = work[spot, :]


def cross_kernel(scale, front_ref, back_ref, raw_ref, ready_ref, out_ref, work):
    is_first = lax.axis_index("probe") == 0

    @pl.when(is_first)
    def _():
        work[...] = products((front_ref, back_ref), (ready_ref, raw_ref)) * scale

    @pl.when(jnp.logical_not(is_first))
    def _():
        work[...] = products((raw_ref, ready_ref), (front_ref, back_ref)) * scale

    in_travelling_order(work, out_ref)


def cross_of(front, back, raw, ready, scale):
    rows = front.shape[1]
    return pl.pallas_call(
        functools.partial(cross_kernel, scale),
        in_specs=[VMEM] * 4,
        out_specs=VMEM,
        out_shape=jax.ShapeDtypeStruct((rows, rows), jnp.float32),
        scratch_shapes=[pltpu.VMEM((rows, rows), jnp.float32)],
        compiler_params=PARAMS,
    )(front, back, raw, ready)


def over_lanes(x, j):
    return jnp.broadcast_to(x[:, j : j + 1], (8, TILE))


def over_rows(x, i):
    return jnp.broadcast_to(x[i : i + 1, :], (8, TILE))


def factor_tile(a_ref, e_ref):
    blocks = TILE // 8
    rows = lax.broadcasted_iota(jnp.int32, (8, TILE), 0)
    lanes = lax.broadcasted_iota(jnp.int32, (8, TILE), 1)
    a = [a_ref[8 * t : 8 * t + 8, :] for t in range(blocks)]

    def repeated(t, s):
        return [over_lanes(a[t], 8 * s + j) for j in range(8)]

    ready = {}
    for s in range(blocks):
        columns = {t: ready[t] if t in ready else repeated(t, s) for t in range(s, blocks)}
        early = range(s + 1, min(s + 1 + EARLY, blocks))
        ready = {t: repeated(t, s + 1) for t in early}
        upper = [over_rows(a[s], k) for k in range(8)]
        side = [jnp.where(lanes < 8 * s, upper[k], jnp.where(lanes == 8 * s + k, 1.0, 0.0)) for k in range(8)]
        for k in range(8):
            pivot = lax.rsqrt(over_rows(columns[s][k], k))
            for t in range(s, blocks):
                columns[t][k] = columns[t][k] * pivot
            upper[k] = upper[k] * pivot
            side[k] = side[k] * pivot
            for m in range(k + 1, 8):
                factor = over_rows(columns[s][k], m)
                for t in range(s, blocks):
                    columns[t][m] = columns[t][m] - columns[t][k] * factor
                upper[m] = upper[m] - upper[k] * factor
                side[m] = side[m] - side[k] * factor
            if s + 1 < blocks:
                for j in range(8):
                    factor = over_rows(columns[s + 1][k], j)
                    for t in early:
                        ready[t][j] = ready[t][j] - columns[t][k] * factor
        done = lanes < 8 * s + 8
        both = [jnp.where(done, side[k], upper[k]) for k in range(8)]
        for t in range(s + 1, blocks):
            a[t] = jnp.where((lanes < 8 * s) | (lanes >= 8 * s + 8), a[t], 0.0)
            for k in range(8):
                a[t] = a[t] - columns[t][k] * both[k]
        for k in range(1, 8):
            upper[0] = jnp.where(rows >= k, upper[k], upper[0])
            side[0] = jnp.where(rows >= k, side[k], side[0])
        a_ref[8 * s : 8 * s + 8, :] = jnp.where(lanes >= rows + 8 * s, upper[0], 0.0)
        e_ref[8 * s : 8 * s + 8, :] = side[0]


def factor_steps(work, r_ref, x_ref, tile_a, tile_e):
    size = work.shape[0]
    blocks = size // TILE
    r_ref[...] = jnp.zeros((size, size), jnp.float32)
    x_ref[...] = jnp.zeros((size, size), jnp.float32)

    def block_step(b, carry):
        spot = pl.ds(pl.multiple_of(b * TILE, TILE), TILE)
        tile_a[...] = work[spot, spot]
        factor_tile(tile_a, tile_e)
        r_ref[spot, spot] = tile_a[...]
        x_ref[spot, spot] = tile_e[...]
        for at in range(blocks):
            here, rest = slice(TILE * at, TILE * at + TILE), slice(TILE * at + TILE, size)

            @pl.when(b == at)
            def _():
                inverse = pieces(tile_e[...])
                if at > 0:
                    done = slice(0, TILE * at)
                    x_ref[here, done] = close_dot(inverse, pieces(x_ref[here, done]), PLAIN)
                if at < blocks - 1:
                    right = close_dot(inverse, pieces(work[here, rest]), PLAIN)
                    r_ref[here, rest] = right
                    right = pieces(right)
                    work[rest, rest] = work[rest, rest] - close_dot(right, right, ACROSS)
                    done = slice(0, TILE * at + TILE)
                    x_ref[rest, done] = x_ref[rest, done] - close_dot(right, pieces(x_ref[here, done]), ACROSS)

        return carry

    lax.fori_loop(0, blocks, block_step, 0)


def factor_scratch(size):
    return [pltpu.VMEM((size, size), jnp.float32)] + [pltpu.VMEM((TILE, TILE), jnp.float32)] * 2


def factor_kernel(g_ref, r_ref, x_ref, work, tile_a, tile_e):
    work[...] = g_ref[...]
    factor_steps(work, r_ref, x_ref, tile_a, tile_e)


def factorize(gram):
    size = gram.shape[0]
    square = jax.ShapeDtypeStruct((size, size), jnp.float32)
    return pl.pallas_call(
        factor_kernel,
        in_specs=[VMEM],
        out_specs=[VMEM, VMEM],
        out_shape=[square, square],
        scratch_shapes=factor_scratch(size),
        compiler_params=PARAMS,
    )(gram)


def pair_kernel(count, g_ref, r_ref, own_ref, other_ref, work, tile_a, tile_e, r_all, x_all):
    rows = r_ref.shape[0]
    share = rows // count
    work[rows:, :rows] = jnp.zeros((rows, rows), jnp.float32)
    for place in range(count):
        start = pl.multiple_of(block_at(place, count) * share, share)
        here = slice(share * place, share * place + share)
        work[pl.ds(start, share), :] = g_ref[here, : 2 * rows]
        work[pl.ds(rows + start, share), rows:] = g_ref[here, 2 * rows :]
    factor_steps(work, r_all, x_all, tile_a, tile_e)
    is_first = lax.axis_index("probe") == 0

    @pl.when(is_first)
    def _():
        r_ref[...] = r_all[:rows, :]
        own_ref[...] = x_all[:rows, :rows]
        other_ref[...] = jnp.zeros((rows, rows), jnp.float32)

    @pl.when(jnp.logical_not(is_first))
    def _():
        r_ref[...] = r_all[rows:, :]
        own_ref[...] = x_all[rows:, rows:]
        other_ref[...] = x_all[rows:, :rows]


def factorize_pair(travelled, count):
    rows = travelled.shape[0]
    square = jax.ShapeDtypeStruct((rows, rows), jnp.float32)
    return pl.pallas_call(
        functools.partial(pair_kernel, count),
        in_specs=[VMEM],
        out_specs=[VMEM] * 3,
        out_shape=[jax.ShapeDtypeStruct((rows, 2 * rows), jnp.float32), square, square],
        scratch_shapes=factor_scratch(2 * rows) + [pltpu.VMEM((2 * rows, 2 * rows), jnp.float32)] * 2,
        compiler_params=PARAMS,
        cost_estimate=taking(15),
    )(travelled)


def basis_kernel(own_ref, other_ref, *refs):
    own_panels, their_panels, (out_ref, held_ref, sems) = refs[:4], refs[4:8], refs[8:]
    me = lax.axis_index("probe")
    quarter = own_panels[0].shape[2]
    own, other = pieces(own_ref[...]), pieces(other_ref[...])
    places = (me * 3, 1 + me, (1 - me) * 2, (1 - me) * 2 + 1)
    copies = [pltpu.make_async_copy(held_ref.at[k], out_ref.at[k], sems.at[k]) for k in range(3)]
    for k in range(3):
        for place, ref in zip(places, own_panels):
            spot = pl.ds(pl.multiple_of(place * quarter, TILE), quarter)
            held_ref[k, :, spot] = close_dot(own, pieces(ref[k]), PLAIN)

        @pl.when(me == 1)
        def _():
            for at, ref in enumerate(their_panels):
                spot = slice(quarter * at, quarter * at + quarter)
                held_ref[k, :, spot] = held_ref[k, :, spot] + close_dot(other, pieces(ref[k]), PLAIN)

        copies[k].start()
    for copy in copies:
        copy.wait()


def basis_of(own, other, *panels):
    _, rows, quarter = panels[0].shape
    shape = (3, rows, 4 * quarter)
    return pl.pallas_call(
        basis_kernel,
        in_specs=[VMEM] * (2 + len(panels)),
        out_specs=pl.BlockSpec(memory_space=pltpu.HBM),
        out_shape=jax.ShapeDtypeStruct(shape, jnp.float32),
        scratch_shapes=[pltpu.VMEM(shape, jnp.float32), pltpu.SemaphoreType.DMA((3,))],
        compiler_params=pltpu.CompilerParams(vmem_limit_bytes=24 * 2**20),
    )(own, other, *panels)


def partners(axis, bit):
    return [(i, i ^ bit) for i in range(lax.axis_size(axis))]


def bits_of(axis):
    bits, bit = [], 1
    while bit < lax.axis_size(axis):
        bits.append(bit)
        bit *= 2
    return bits


def split_bits(axis):
    bits = bits_of(axis)
    return bits[: max(len(bits) - 2, 0)], bits[max(len(bits) - 2, 0) :]


def scatter_sum(block, axis):
    halved, whole = split_bits(axis)
    for bit in halved:
        half = block.shape[0] // 2
        block = block[:half] + lax.ppermute(block[half:], axis, partners(axis, bit))
    for bit in whole:
        block = block + lax.ppermute(block, axis, partners(axis, bit))
    return block


def gather_back(block, axis):
    for bit in reversed(split_bits(axis)[0]):
        block = jnp.concatenate([block, lax.ppermute(block, axis, partners(axis, bit))], 0)
    return block


def swapped(block):
    return lax.ppermute(block, "probe", [(0, 1), (1, 0)])


def halo_of(first, last):
    slabs = lax.axis_size("slab")
    forward = [(i, i + 1) for i in range(slabs - 1)]
    return lax.ppermute(last, "slab", forward), lax.ppermute(first, "slab", [(b, a) for a, b in forward])


def pair_body(probes, coefs, first, mid, last, offsets):
    _, columns, cells = probes.shape
    slabs = lax.axis_size("slab")
    scale = 1.0 / (3 * cells * slabs)
    me = lax.axis_index("probe")
    is_first = me == 0
    quarter = cells // 4
    tiles = quarter // TILE

    low, high = halo_of(first, last)
    pack = 3 * HALO
    ends = swapped(
        jnp.where(
            is_first,
            jnp.concatenate([low[:pack], mid[:pack]], 0),
            jnp.concatenate([mid[:pack], high[:pack]], 0),
        )
    )
    theirs = swapped(lax.dynamic_slice_in_dim(probes, me * 3 * quarter, quarter, 2))
    run = functools.partial(segment, offsets=offsets, coefs=coefs)

    def at_half(me):
        return me * 2 * tiles

    def at_other_half(me):
        return (1 - me) * 2 * tiles

    def at_raw(me):
        return (1 - me) * 3 * tiles

    edges = (low, high)
    outer, inner = run(at_half, at_half, 2 * tiles, x=probes, edges=edges, parts=2, inward=True)
    inner, ends = lax.optimization_barrier((inner, ends))
    ready = swapped(inner)
    front, back, gram = run(
        at_other_half, at_other_half, 2 * tiles, x=probes, edges=edges, parts=2, rest=(inner, outer), scale=scale
    )
    early = swapped(front)
    raw = run(lambda me: 0, at_raw, tiles, x=theirs, edges=edges, ends=ends)
    count = 1 << len(split_bits("slab")[0])
    cross = cross_of(front, back, raw, ready, scale)
    own, cross = scatter_sum(gram, "slab"), scatter_sum(cross, "slab")
    own, cross, early = lax.optimization_barrier((own, cross, early))
    their_own, their_cross = swapped(own), swapped(cross)
    their_own, their_cross, late = lax.optimization_barrier((their_own, their_cross, back))
    late = swapped(late)
    share = jnp.concatenate(
        [jnp.where(is_first, own, their_own), cross + their_cross, jnp.where(is_first, their_own, own)], 1
    )
    r_rows, own, other = factorize_pair(gather_back(share, "slab"), count)
    return basis_of(own, other, outer, inner, front, back, raw, ready, early, late), r_rows


def whole_body(probes, coefs, first, mid, last, offsets):
    _, columns, cells = probes.shape
    slabs = lax.axis_size("slab")
    me = lax.axis_index("probe")
    scale = 1.0 / (3 * cells * slabs)
    low, high = halo_of(first, last)
    panel = segment(lambda me: 0, lambda me: 0, cells // TILE, offsets, probes, coefs, (low, high))
    everyone = lax.all_gather(panel, "probe", axis=1, tiled=True)
    part = scale * jnp.einsum("kpc,kqc->pq", panel, everyone, precision=CLOSE)
    gram = lax.all_gather(lax.psum(part, "slab"), "probe", axis=0, tiled=True)
    upper, inverse = factorize(gram)
    mine = lax.dynamic_slice_in_dim(inverse, me * columns, columns, 0)
    basis = jnp.einsum("pq,kqc->kpc", mine, everyone, precision=CLOSE)
    return basis, lax.dynamic_slice_in_dim(upper, me * columns, columns, 0)


def body(probes, viscosity, coupling, misfit_weight, band_offsets):
    first, mid, last, coefs = pack_edges(probes, coupling, viscosity, misfit_weight)
    run = pair_body if lax.axis_size("probe") == 2 else whole_body
    return run(probes, coefs, first, mid, last, band_offsets)


def solution(mesh):
    return jax.shard_map(
        body,
        mesh=mesh,
        in_specs=(
            P(None, "probe", "slab"),
            P("slab"),
            P(None, None, None, "slab"),
            P(None, "slab"),
            P(),
        ),
        out_specs=(P(None, "probe", "slab"), P("probe", None)),
        check_vma=False,
    )
```
